32 devices in a mesh: ep: 4 (over y, x), sp: 8 (over z, core).
Axes of the slice: x: 2, y: 2, z: 4, core: 2. Of those that a mesh axis runs over, the one named last changes fastest.
Arguments:
- grad_out: bfloat16 [4096, 4096], P(('ep', 'sp')), may hold values from -1.5 to 1.5
- routes: int32 [4096, 8], P(('ep', 'sp')), may hold values from 0 to 127, as said below
- gate: bfloat16 [4096, 8], P(('ep', 'sp')), may hold values from 0.049804688 to 1
- saved: bfloat16 [4, 8, 64, 3072], P('ep', 'sp'), may hold values from -6 to 6
- w_down: bfloat16 [4, 1536, 4096], P('ep', None, 'sp'), may hold values from -0.15625 to 0.15625
Outputs:
- grad_pre: bfloat16 [4, 8, 64, 3072], P('ep', 'sp')
- grad_gate: float32 [4096, 8], P(('ep', 'sp'))
The draws below stay inside these ranges and needn't reach their ends.
Inputs may be any that keep to these rules, and one draw needn't show every extreme that they name: `routes`: each row names 8 different experts. In every block of 128 rows at most 16 rows name the same expert whose number is a multiple of 32, and in every block one such expert is named by exactly 16 rows; it is the same expert for all blocks whose indices agree modulo 8.
All inputs are finite; a program needn't handle non-finite values.
Results may differ from the reference program's by a relative error of at most 0.0029.
Values may be sent and summed in bfloat16 or wider, within the bound.
A program may use at most 128 MiB of HBM per device.

```python
import jax
import jax.numpy as jnp
from jax import lax

D = 4096
FF = 1536
EXPERTS = 128
TOP = 8
TOK_DEV = 128
CAP = 16
EXP_DEV = 32
WAVE = 4
SPLITS = 8
TOKENS = 4096


def draw_routes(key, part):
    flights = EXPERTS // EXP_DEV
    blocks = TOKENS // TOK_DEV
    split_count = blocks // flights
    subkeys = jax.random.split(jax.random.fold_in(key, 17), 5)
    heat_level = jax.random.randint(subkeys[0], (flights,), 0, 4)
    base_count = jax.random.randint(subkeys[1], (blocks, flights), 0, CAP // 2 + 1)
    counts = jnp.minimum(base_count * (heat_level[None, :] + 1), CAP)
    chosen = jax.random.randint(subkeys[2], (split_count,), 0, flights)
    forced = jnp.tile(chosen, blocks // split_count)
    is_forced = jnp.arange(flights)[None, :] == forced[:, None]
    counts = jnp.where(is_forced, CAP, counts)
    rank_raw = jax.random.randint(subkeys[3], (blocks, flights, TOK_DEV), 0, 1 << 16) * TOK_DEV + jnp.arange(TOK_DEV)[None, None, :]
    ordering = jnp.argsort(rank_raw, axis=2)
    rank_of = jnp.argsort(ordering, axis=2)
    picked = rank_of < counts[:, :, None]
    member = jnp.transpose(picked, (0, 2, 1)).reshape(TOKENS, flights)
    forced_tok = jnp.transpose(picked & is_forced[:, :, None], (0, 2, 1)).reshape(TOKENS, flights)
    expert_numbers = jnp.arange(EXPERTS)
    score_values = jax.random.randint(subkeys[4], (TOKENS, EXPERTS), 0, 1 << 16) * EXPERTS + expert_numbers[None, :]
    in_wave = expert_numbers % EXP_DEV == 0
    wave_of = expert_numbers // EXP_DEV
    membership_per_expert = jnp.take(member, wave_of, axis=1)
    compelled_per_expert = jnp.take(forced_tok, wave_of, axis=1).astype(jnp.int32)
    extra_length = 1 << 24
    wave_routing_scores = jnp.where(membership_per_expert, extra_length + compelled_per_expert * extra_length + score_values, -1 - expert_numbers[None, :])
    score_values = jnp.where(in_wave[None, :], wave_routing_scores, score_values)
    top_values, routes = lax.top_k(score_values, TOP)
    return routes.astype(jnp.int32)


def shard_levels(stream_key, shape, cuts, smallest, top_value):
    def one(axis_at, blocks):
        steps = jax.random.uniform(jax.random.fold_in(jax.random.fold_in(stream_key, 6), axis_at), (blocks,), jnp.float32, smallest / len(cuts), top_value / len(cuts))
        return jnp.repeat(jnp.exp(steps), shape[axis_at] // blocks).reshape((-1,) + (1,) * (len(shape) - axis_at - 1))

    level = one(*cuts[0])
    for cut in cuts[1:]:
        level = level * one(*cut)
    return level


def noise(own_key, extent, width, most, shards=(), kind=jnp.bfloat16):
    drawn = width * jax.random.normal(own_key, extent, jnp.float32)
    if shards:
        drawn = drawn * shard_levels(own_key, extent, shards, -0.22, 0.18)
    return jnp.clip(drawn, -most, most).astype(kind)


def setup_inputs(seed: int = 0) -> dict:
    key_list = jax.random.split(jax.random.key(seed), 6)
    grad_out = noise(key_list[0], (TOKENS, D), 0.25, 1.5, ((0, 32),))
    routes = draw_routes(jax.random.fold_in(key_list[5], 71), 0)
    gate = jnp.clip(0.049804688 + 0.9501953 * jax.random.uniform(key_list[2], (TOKENS, TOP), jnp.float32) ** shard_levels(key_list[2], (TOKENS, TOP), ((0, 32),), -0.2, 0.2), 0.049804688, 1.0).astype(jnp.bfloat16)
    saved = noise(key_list[3], (WAVE, SPLITS, WAVE * CAP, 2 * FF), 1.0, 6.0, ((0, 4), (1, 8)))
    w_down = noise(key_list[4], (WAVE, FF, D), FF ** -0.5, 0.15625, ((0, 4), (2, 8)))
    return dict(grad_out=grad_out, routes=routes, gate=gate, saved=saved, w_down=w_down)


def reference(grad_out, routes, gate, saved, w_down):
    flight = (routes % EXP_DEV) == 0
    owners = (routes // EXP_DEV).astype(jnp.int32)
    wave_ids = jnp.arange(WAVE, dtype=jnp.int32)
    onehot = (owners[:, :, None] == wave_ids[None, None, :]) & flight[:, :, None]
    member = jnp.sum(onehot.astype(jnp.int32), axis=1)
    gate_by_expert = jnp.sum(onehot.astype(jnp.float32) * gate.astype(jnp.float32)[:, :, None], axis=1)
    blocked_rows = member.reshape(TOKENS // TOK_DEV, TOK_DEV, WAVE)
    places = (jnp.cumsum(blocked_rows, axis=1) - blocked_rows).reshape(TOKENS, WAVE).astype(jnp.int32)
    token_ids = jnp.arange(TOKENS, dtype=jnp.int32)
    block_index = token_ids // TOK_DEV
    source = block_index // SPLITS
    split_index = block_index % SPLITS
    per_expert = SPLITS * WAVE * CAP
    slot_total = WAVE * per_expert
    position = wave_ids[None, :] * per_expert + (split_index[:, None] * WAVE + source[:, None]) * CAP + places
    position = position.astype(jnp.int32)
    target = jnp.where(member > 0, position, slot_total).reshape(-1)
    token_table = jnp.full((slot_total,), TOKENS, jnp.int32).at[target].set(
        jnp.broadcast_to(token_ids[:, None], (TOKENS, WAVE)).reshape(-1), mode="drop")
    gate_table = jnp.zeros((slot_total,), jnp.float32).at[target].set(gate_by_expert.reshape(-1), mode="drop")
    padded = jnp.concatenate([grad_out, jnp.zeros((1, D), grad_out.dtype)], axis=0)

    def one_expert(inputs):
        weight, tokens_here, gates_here, saved_here = inputs
        arrived = padded[tokens_here].astype(jnp.float32)
        grad_hidden = lax.dot_general(arrived, weight.astype(jnp.float32), (((1,), (1,)), ((), ())),
                                      precision=lax.Precision.HIGHEST)
        flat_saved = saved_here.reshape(per_expert, 2 * FF)
        gate_pre = flat_saved[:, :FF].astype(jnp.float32)
        up_pre = flat_saved[:, FF:].astype(jnp.float32)
        sigmoid_gate = jax.nn.sigmoid(gate_pre)
        silu_gate = gate_pre * sigmoid_gate
        hidden = (silu_gate * up_pre).astype(jnp.bfloat16)
        score_values = jnp.sum(grad_hidden * lax.optimization_barrier(hidden).astype(jnp.float32), axis=1)
        scaled = grad_hidden * gates_here[:, None]
        grad_gate_pre = scaled * up_pre * sigmoid_gate * (1.0 + gate_pre * (1.0 - sigmoid_gate))
        grad_up_pre = scaled * silu_gate
        grad_pre = jnp.concatenate([grad_gate_pre, grad_up_pre], axis=1).astype(jnp.bfloat16)
        return grad_pre.reshape(SPLITS, WAVE * CAP, 2 * FF), score_values

    grad_pre, score_values = lax.map(one_expert, (w_down, token_table.reshape(WAVE, per_expert),
                                            gate_table.reshape(WAVE, per_expert), saved))
    route_position = jnp.take_along_axis(position, owners, axis=1)
    routing_weights = score_values.reshape(-1)[jnp.clip(route_position, 0, slot_total - 1)]
    grad_gate = jnp.where(flight, routing_weights, jnp.zeros_like(routing_weights))
    return grad_pre, grad_gate
```

```python
import functools

import jax
import jax.numpy as jnp
from jax import lax
from jax.experimental import pallas as pl
from jax.experimental.pallas import tpu as pltpu
from jax.sharding import PartitionSpec as P

EXPERTS = 128
MESH = pl.DeviceIdType.MESH
F32 = jnp.float32
BF16 = jnp.bfloat16


def loop(count, body):
    if count <= 4:
        for i in range(count):
            body(i)
    else:

        @pl.loop(0, count)
        def _(i):
            body(i)


def kernel(
    ep,
    chips,
    routes_ref,
    gate_ref,
    grad_ref,
    saved_ref,
    w_ref,
    pre_ref,
    gg_ref,
    grad_v,
    saved_v,
    wbuf,
    rows_out,
    rows_in,
    gate_out,
    gate_in,
    part_out,
    part_in,
    score_out,
    score_in,
    own,
    hid,
    fa,
    fu,
    pre_v,
    load_sem,
    w_sem,
    row_sem,
    gate_sem,
    part_sem,
    score_sem,
    local_sem,
):
    tokens, top = routes_ref.shape
    cap = rows_out.shape[2]
    cols = rows_out.shape[3]
    slots = ep * cap
    ff = w_ref.shape[0]
    kw = w_ref.shape[1]
    me_e = lax.axis_index("ep")
    me_s = lax.axis_index("sp")
    me_z = me_s // 2
    me_c = me_s % 2
    sibling = me_z * 2 + (1 - me_c)

    load_grad = pltpu.make_async_copy(grad_ref, grad_v, load_sem.at[0])
    load_grad.start()
    load_w = pltpu.make_async_copy(w_ref, wbuf.at[me_c], load_sem.at[1])
    load_w.start()
    load_saved = pltpu.make_async_copy(saved_ref, saved_v, load_sem.at[2])
    load_saved.start()

    barrier = pltpu.get_barrier_semaphore()
    pl.semaphore_signal(barrier, inc=1, device_id=(me_e, sibling), device_id_type=MESH)

    def greet(k):
        e = lax.rem(me_e + k // chips, ep)
        z = lax.rem(me_z + k % chips, chips)
        pl.semaphore_signal(barrier, inc=1, device_id=(e, z * 2 + me_c), device_id_type=MESH)

    @pl.loop(1, ep * chips)
    def _(k):
        greet(k)

    step = EXPERTS // ep
    routes = routes_ref[...]
    gates = gate_ref[...].astype(F32)
    slot_id = lax.broadcasted_iota(jnp.int32, (slots, tokens), 0)
    place_id = (slot_id % cap).astype(F32)
    ones = jnp.ones((cap, top), F32)
    members, weights = [], []
    nt = (((1,), (1,)), ((), ()))
    for f in range(ep):
        hit = (routes == f * step).astype(F32)
        members.append(lax.dot_general(ones, hit, nt, preferred_element_type=F32))
        weights.append(lax.dot_general(ones, hit * gates, nt, preferred_element_type=F32))
    member = jnp.concatenate(members, axis=0)
    weight = jnp.concatenate(weights, axis=0)
    before = (
        lax.broadcasted_iota(jnp.int32, (tokens, tokens), 0)
        < lax.broadcasted_iota(jnp.int32, (tokens, tokens), 1)
    ).astype(F32)
    place = jnp.dot(member.astype(BF16), before.astype(BF16), preferred_element_type=F32)
    chosen = jnp.where((place == place_id) & (member > 0.5), 1.0, 0.0)
    picked = jnp.sum(chosen * weight, axis=1, keepdims=True)
    gate_out[...] = jnp.broadcast_to(picked, (slots, 128)).reshape(ep, cap, 128)
    chosen16 = chosen.astype(BF16)

    load_grad.wait()
    pl.semaphore_wait(barrier, ep * chips)

    w_copy = pltpu.make_async_remote_copy(
        src_ref=w_ref,
        dst_ref=wbuf.at[me_c],
        send_sem=w_sem.at[0],
        recv_sem=w_sem.at[1],
        device_id=(me_e, sibling),
        device_id_type=MESH,
    )
    w_copy.start()

    def row_copy(e, z):
        return pltpu.make_async_remote_copy(
            src_ref=rows_out.at[z, e],
            dst_ref=rows_in.at[me_z, me_e],
            send_sem=row_sem.at[0, z, e],
            recv_sem=row_sem.at[1, me_z, me_e],
            device_id=(e, z * 2 + me_c),
            device_id_type=MESH,
        )

    def row_arrival(e, z):
        return pltpu.make_async_remote_copy(
            src_ref=rows_out.at[me_z, me_e],
            dst_ref=rows_in.at[z, e],
            send_sem=row_sem.at[0, me_z, me_e],
            recv_sem=row_sem.at[1, z, e],
            device_id=(e, z * 2 + me_c),
            device_id_type=MESH,
        )

    def gate_copy(e):
        return pltpu.make_async_remote_copy(
            src_ref=gate_out.at[e],
            dst_ref=gate_in.at[me_e],
            send_sem=gate_sem.at[0, e],
            recv_sem=gate_sem.at[1, me_e],
            device_id=(e, me_s),
            device_id_type=MESH,
        )

    def gate_arrival(e):
        return pltpu.make_async_remote_copy(
            src_ref=gate_out.at[me_e],
            dst_ref=gate_in.at[e],
            send_sem=gate_sem.at[0, me_e],
            recv_sem=gate_sem.at[1, e],
            device_id=(e, me_s),
            device_id_type=MESH,
        )

    def score_copy(e):
        return pltpu.make_async_remote_copy(
            src_ref=score_out.at[e],
            dst_ref=score_in.at[me_e],
            send_sem=score_sem.at[0, e],
            recv_sem=score_sem.at[1, me_e],
            device_id=(e, me_s),
            device_id_type=MESH,
        )

    def score_arrival(e):
        return pltpu.make_async_remote_copy(
            src_ref=score_out.at[me_e],
            dst_ref=score_in.at[e],
            send_sem=score_sem.at[0, me_e],
            recv_sem=score_sem.at[1, e],
            device_id=(e, me_s),
            device_id_type=MESH,
        )

    def part_copy(z):
        return pltpu.make_async_remote_copy(
            src_ref=part_out.at[z],
            dst_ref=part_in.at[me_z],
            send_sem=part_sem.at[0, z],
            recv_sem=part_sem.at[1, me_z],
            device_id=(me_e, z * 2 + me_c),
            device_id_type=MESH,
        )

    def part_arrival(z):
        return pltpu.make_async_remote_copy(
            src_ref=part_out.at[me_z],
            dst_ref=part_in.at[z],
            send_sem=part_sem.at[0, me_z],
            recv_sem=part_sem.at[1, z],
            device_id=(me_e, z * 2 + me_c),
            device_id_type=MESH,
        )

    keep_rows = pltpu.make_async_copy(
        rows_out.at[me_z, me_e], rows_in.at[me_z, me_e], local_sem.at[0]
    )
    keep_gate = pltpu.make_async_copy(gate_out.at[me_e], gate_in.at[me_e], local_sem.at[1])
    keep_score = pltpu.make_async_copy(score_out.at[me_e], score_in.at[me_e], local_sem.at[2])

    def send_rows(i):
        z = lax.rem(me_z + i + 1, chips)
        block = jnp.dot(
            chosen16,
            grad_v[:, pl.ds(pl.multiple_of(z * cols, cols), cols)],
            preferred_element_type=F32,
        )
        rows_out[z] = block.astype(BF16).reshape(ep, cap, cols)

        def one(k):
            e = lax.rem(me_e + k, ep)

            @pl.when((e != me_e) | (z != me_z))
            def _():
                row_copy(e, z).start()

        loop(ep, one)

    loop(chips, send_rows)
    keep_rows.start()
    keep_gate.start()

    @pl.loop(1, ep)
    def _(k):
        gate_copy(lax.rem(me_e + k, ep)).start()

    load_saved.wait()
    block_rows = 16

    @pl.loop(0, slots // block_rows)
    def _(i):
        at = pl.ds(pl.multiple_of(i * block_rows, block_rows), block_rows)
        a = saved_v[at, :ff].astype(F32)
        u = saved_v[at, ff:].astype(F32)
        sig = jax.nn.sigmoid(a)
        silu = a * sig
        hid[at, :] = (silu * u).astype(BF16)
        fa[at, :] = u * sig * (1.0 + a * (1.0 - sig))
        fu[at, :] = silu

    load_w.wait()
    w_copy.wait()

    def times_w(z):
        rows = rows_in[z].reshape(slots, cols)
        return lax.dot_general(
            rows[:, :kw], wbuf[0], nt, preferred_element_type=F32
        ) + lax.dot_general(rows[:, kw:], wbuf[1], nt, preferred_element_type=F32)

    def wait_rows(z):
        def one(k):
            e = lax.rem(me_e + k, ep)

            @pl.when((e != me_e) | (z != me_z))
            def _():
                row_arrival(e, z).wait_recv()

        loop(ep, one)

    def send_part(i):
        z = lax.rem(me_z + chips - 1 - i, chips)
        wait_rows(z)
        part_out[z] = times_w(z).astype(BF16)
        part_copy(z).start()

    loop(chips - 1, send_part)
    wait_rows(me_z)
    keep_rows.wait()
    own[...] = times_w(me_z)

    def add_part(i):
        z = lax.rem(me_z + i + 1, chips)
        part_arrival(z).wait_recv()

        @pl.loop(0, slots // block_rows)
        def _(j):
            at = pl.ds(pl.multiple_of(j * block_rows, block_rows), block_rows)
            own[at, :] += part_in[z, at, :].astype(F32)

    loop(chips - 1, add_part)

    keep_gate.wait()

    @pl.loop(1, ep)
    def _(k):
        gate_arrival(lax.rem(me_e + k, ep)).wait_recv()

    @pl.loop(0, ep)
    def _(e):
        at = pl.ds(pl.multiple_of(e * cap, cap), cap)
        score = jnp.sum(own[at, :] * hid[at, :].astype(F32), axis=1, keepdims=True)
        score_out[e] = jnp.broadcast_to(score, (cap, 128))

    @pl.loop(1, ep)
    def _(k):
        score_copy(lax.rem(me_e + k, ep)).start()

    keep_score.start()

    @pl.loop(0, ep)
    def _(e):
        at = pl.ds(pl.multiple_of(e * cap, cap), cap)
        scaled = own[at, :] * gate_in[e][:, :1]
        pre_v[at, :ff] = (scaled * fa[at, :]).astype(BF16)
        pre_v[at, ff:] = (scaled * fu[at, :]).astype(BF16)

    store = pltpu.make_async_copy(pre_v, pre_ref, load_sem.at[0])
    store.start()

    keep_score.wait()

    @pl.loop(1, ep)
    def _(k):
        score_arrival(lax.rem(me_e + k, ep)).wait_recv()

    got = score_in[...].reshape(slots, 128)
    spread = jnp.sum((chosen * got[:, :1]).reshape(ep, cap, tokens), axis=1)
    pad = -ep % 8
    if pad:
        spread = jnp.concatenate([spread, jnp.zeros((pad, tokens), F32)], axis=0)
    by_token = spread.T
    result = jnp.zeros((tokens, top), F32)
    for f in range(ep):
        result += jnp.where(routes == f * step, by_token[:, f : f + 1], 0.0)
    gg_ref[...] = result

    def sent(k):
        e = lax.rem(me_e + k // chips, ep)
        z = lax.rem(me_z + k % chips, chips)
        row_copy(e, z).wait_send()

    @pl.loop(1, ep * chips)
    def _(k):
        sent(k)

    @pl.loop(1, ep)
    def _(k):
        e = lax.rem(me_e + k, ep)
        gate_copy(e).wait_send()
        score_copy(e).wait_send()

    @pl.loop(1, chips)
    def _(k):
        part_copy(lax.rem(me_z + k, chips)).wait_send()

    store.wait()


def on_device(ep, sp, grad_out, routes, gate, saved, w_down):
    tokens, width = grad_out.shape
    slots = saved.shape[2]
    ff = saved.shape[3] // 2
    kw = w_down.shape[2]
    cap = slots // ep
    chips = sp // 2
    cols = 2 * kw
    vmem = pl.BlockSpec(memory_space=pltpu.VMEM)
    hbm = pl.BlockSpec(memory_space=pl.ANY)
    pre, grad_gate = pl.pallas_call(
        functools.partial(kernel, ep, chips),
        out_shape=(
            jax.ShapeDtypeStruct((slots, 2 * ff), BF16),
            jax.ShapeDtypeStruct((tokens, routes.shape[1]), F32),
        ),
        in_specs=[vmem, vmem, hbm, hbm, hbm],
        out_specs=(hbm, vmem),
        scratch_shapes=[
            pltpu.VMEM((tokens, width), BF16),
            pltpu.VMEM((slots, 2 * ff), BF16),
            pltpu.VMEM((2, ff, kw), BF16),
            pltpu.VMEM((chips, ep, cap, cols), BF16),
            pltpu.VMEM((chips, ep, cap, cols), BF16),
            pltpu.VMEM((ep, cap, 128), F32),
            pltpu.VMEM((ep, cap, 128), F32),
            pltpu.VMEM((chips, slots, ff), BF16),
            pltpu.VMEM((chips, slots, ff), BF16),
            pltpu.VMEM((ep, cap, 128), F32),
            pltpu.VMEM((ep, cap, 128), F32),
            pltpu.VMEM((slots, ff), F32),
            pltpu.VMEM((slots, ff), BF16),
            pltpu.VMEM((slots, ff), F32),
            pltpu.VMEM((slots, ff), F32),
            pltpu.VMEM((slots, 2 * ff), BF16),
            pltpu.SemaphoreType.DMA((3,)),
            pltpu.SemaphoreType.DMA((2,)),
            pltpu.SemaphoreType.DMA((2, chips, ep)),
            pltpu.SemaphoreType.DMA((2, ep)),
            pltpu.SemaphoreType.DMA((2, chips)),
            pltpu.SemaphoreType.DMA((2, ep)),
            pltpu.SemaphoreType.DMA((3,)),
        ],
        compiler_params=pltpu.CompilerParams(
            collective_id=0, has_side_effects=True, vmem_limit_bytes=56 * 1024 * 1024
        ),
    )(routes, gate, grad_out, saved.reshape(slots, 2 * ff), w_down.reshape(ff, kw))
    return pre.reshape(saved.shape), grad_gate


def solution(mesh):
    ep, sp = mesh.shape["ep"], mesh.shape["sp"]
    in_specs = (
        P(("ep", "sp"), None),
        P(("ep", "sp"), None),
        P(("ep", "sp"), None),
        P("ep", "sp", None, None),
        P("ep", None, "sp"),
    )
    out_specs = (P("ep", "sp", None, None), P(("ep", "sp"), None))
    return jax.shard_map(
        functools.partial(on_device, ep, sp),
        mesh=mesh,
        in_specs=in_specs,
        out_specs=out_specs,
        check_vma=False,
    )
```

```python
import functools

import jax
import jax.numpy as jnp
from jax import lax
from jax.experimental import pallas as pl
from jax.experimental.pallas import tpu as pltpu
from jax.sharding import PartitionSpec as P

EXPERTS = 128
MESH = pl.DeviceIdType.MESH
F32 = jnp.float32
BF16 = jnp.bfloat16


def loop(count, body):
    if count <= 4:
        for i in range(count):
            body(i)
    else:

        @pl.loop(0, count)
        def _(i):
            body(i)


def kernel(
    ep,
    chips,
    routes_ref,
    gate_ref,
    grad_ref,
    saved_ref,
    w_ref,
    pre_ref,
    gg_ref,
    grad_v,
    saved_v,
    wbuf,
    rows_out,
    rows_in,
    gate_out,
    gate_in,
    part_out,
    part_in,
    score_out,
    score_in,
    own,
    hid,
    fa,
    fu,
    pre_v,
    load_sem,
    w_sem,
    row_sem,
    gate_sem,
    part_sem,
    score_sem,
    local_sem,
):
    top, tokens = routes_ref.shape
    nt = (((1,), (1,)), ((), ()))
    cap = rows_out.shape[2]
    cols = rows_out.shape[3]
    slots = ep * cap
    ff = w_ref.shape[0]
    kw = w_ref.shape[1]
    me_e = lax.axis_index("ep")
    me_s = lax.axis_index("sp")
    me_z = me_s // 2
    me_c = me_s % 2
    sibling = me_z * 2 + (1 - me_c)

    load_grad = pltpu.make_async_copy(grad_ref, grad_v, load_sem.at[0])
    load_grad.start()
    load_w = pltpu.make_async_copy(w_ref, wbuf.at[me_c], load_sem.at[1])
    load_w.start()
    load_saved = pltpu.make_async_copy(saved_ref, saved_v, load_sem.at[2])
    load_saved.start()

    barrier = pltpu.get_barrier_semaphore()
    pl.semaphore_signal(barrier, inc=1, device_id=(me_e, sibling), device_id_type=MESH)

    def greet(k):
        e = lax.rem(me_e + k // chips, ep)
        z = lax.rem(me_z + k % chips, chips)
        pl.semaphore_signal(barrier, inc=1, device_id=(e, z * 2 + me_c), device_id_type=MESH)

    @pl.loop(1, ep * chips)
    def _(k):
        greet(k)

    step = EXPERTS // ep
    routes = routes_ref[...]
    gates = gate_ref[...].astype(F32)
    slot_id = lax.broadcasted_iota(jnp.int32, (slots, tokens), 0)
    place_id = (slot_id % cap).astype(F32)
    members, weights = [], []
    for f in range(ep):
        hit = (routes == f * step).astype(F32)
        count = jnp.sum(hit, axis=0, keepdims=True)
        value = jnp.sum(hit * gates, axis=0, keepdims=True)
        members.append(jnp.broadcast_to(count, (cap, tokens)))
        weights.append(jnp.broadcast_to(value, (cap, tokens)))
    member = jnp.concatenate(members, axis=0)
    weight = jnp.concatenate(weights, axis=0)
    before = (
        lax.broadcasted_iota(jnp.int32, (tokens, tokens), 0)
        < lax.broadcasted_iota(jnp.int32, (tokens, tokens), 1)
    ).astype(F32)
    place = jnp.dot(member.astype(BF16), before.astype(BF16), preferred_element_type=F32)
    chosen = jnp.where((place == place_id) & (member > 0.5), 1.0, 0.0)
    picked = jnp.sum(chosen * weight, axis=1, keepdims=True)
    gate_out[...] = jnp.broadcast_to(picked, (slots, 128)).reshape(ep, cap, 128)
    chosen16 = chosen.astype(BF16)

    load_grad.wait()
    pl.semaphore_wait(barrier, ep * chips)

    w_copy = pltpu.make_async_remote_copy(
        src_ref=w_ref,
        dst_ref=wbuf.at[me_c],
        send_sem=w_sem.at[0],
        recv_sem=w_sem.at[1],
        device_id=(me_e, sibling),
        device_id_type=MESH,
    )
    w_copy.start()

    def row_copy(e, z):
        return pltpu.make_async_remote_copy(
            src_ref=rows_out.at[z, e],
            dst_ref=rows_in.at[me_z, me_e],
            send_sem=row_sem.at[0, z, e],
            recv_sem=row_sem.at[1, me_z, me_e],
            device_id=(e, z * 2 + me_c),
            device_id_type=MESH,
        )

    def row_arrival(e, z):
        return pltpu.make_async_remote_copy(
            src_ref=rows_out.at[me_z, me_e],
            dst_ref=rows_in.at[z, e],
            send_sem=row_sem.at[0, me_z, me_e],
            recv_sem=row_sem.at[1, z, e],
            device_id=(e, z * 2 + me_c),
            device_id_type=MESH,
        )

    def gate_copy(e):
        return pltpu.make_async_remote_copy(
            src_ref=gate_out.at[e],
            dst_ref=gate_in.at[me_e],
            send_sem=gate_sem.at[0, e],
            recv_sem=gate_sem.at[1, me_e],
            device_id=(e, me_s),
            device_id_type=MESH,
        )

    def gate_arrival(e):
        return pltpu.make_async_remote_copy(
            src_ref=gate_out.at[me_e],
            dst_ref=gate_in.at[e],
            send_sem=gate_sem.at[0, me_e],
            recv_sem=gate_sem.at[1, e],
            device_id=(e, me_s),
            device_id_type=MESH,
        )

    def score_copy(e):
        return pltpu.make_async_remote_copy(
            src_ref=score_out.at[e],
            dst_ref=score_in.at[me_e],
            send_sem=score_sem.at[0, e],
            recv_sem=score_sem.at[1, me_e],
            device_id=(e, me_s),
            device_id_type=MESH,
        )

    def score_arrival(e):
        return pltpu.make_async_remote_copy(
            src_ref=score_out.at[me_e],
            dst_ref=score_in.at[e],
            send_sem=score_sem.at[0, me_e],
            recv_sem=score_sem.at[1, e],
            device_id=(e, me_s),
            device_id_type=MESH,
        )

    def part_copy(z):
        return pltpu.make_async_remote_copy(
            src_ref=part_out.at[z],
            dst_ref=part_in.at[me_z],
            send_sem=part_sem.at[0, z],
            recv_sem=part_sem.at[1, me_z],
            device_id=(me_e, z * 2 + me_c),
            device_id_type=MESH,
        )

    def part_arrival(z):
        return pltpu.make_async_remote_copy(
            src_ref=part_out.at[me_z],
            dst_ref=part_in.at[z],
            send_sem=part_sem.at[0, me_z],
            recv_sem=part_sem.at[1, z],
            device_id=(me_e, z * 2 + me_c),
            device_id_type=MESH,
        )

    keep_rows = pltpu.make_async_copy(
        rows_out.at[me_z, me_e], rows_in.at[me_z, me_e], local_sem.at[0]
    )
    keep_gate = pltpu.make_async_copy(gate_out.at[me_e], gate_in.at[me_e], local_sem.at[1])
    keep_score = pltpu.make_async_copy(score_out.at[me_e], score_in.at[me_e], local_sem.at[2])

    def send_rows(i):
        z = lax.rem(me_z + i + 1, chips)
        block = jnp.dot(
            chosen16,
            grad_v[:, pl.ds(pl.multiple_of(z * cols, cols), cols)],
            preferred_element_type=F32,
        )
        rows_out[z] = block.astype(BF16).reshape(ep, cap, cols)

        def one(k):
            e = lax.rem(me_e + k, ep)

            @pl.when((e != me_e) | (z != me_z))
            def _():
                row_copy(e, z).start()

        loop(ep, one)

    loop(chips, send_rows)
    keep_rows.start()
    keep_gate.start()

    @pl.loop(1, ep)
    def _(k):
        gate_copy(lax.rem(me_e + k, ep)).start()

    load_saved.wait()
    block_rows = 16

    @pl.loop(0, slots // block_rows)
    def _(i):
        at = pl.ds(pl.multiple_of(i * block_rows, block_rows), block_rows)
        a = saved_v[at, :ff].astype(F32)
        u = saved_v[at, ff:].astype(F32)
        sig = jax.nn.sigmoid(a)
        silu = a * sig
        hid[at, :] = (silu * u).astype(BF16)
        fa[at, :] = u * sig * (1.0 + a * (1.0 - sig))
        fu[at, :] = silu

    load_w.wait()
    w_copy.wait()

    def times_w(z):
        rows = rows_in[z].reshape(slots, cols)
        return lax.dot_general(
            rows[:, :kw], wbuf[0], nt, preferred_element_type=F32
        ) + lax.dot_general(rows[:, kw:], wbuf[1], nt, preferred_element_type=F32)

    def wait_rows(z):
        def one(k):
            e = lax.rem(me_e + k, ep)

            @pl.when((e != me_e) | (z != me_z))
            def _():
                row_arrival(e, z).wait_recv()

        loop(ep, one)

    def send_part(i):
        z = lax.rem(me_z + chips - 1 - i, chips)
        wait_rows(z)
        part_out[z] = times_w(z).astype(BF16)
        part_copy(z).start()

    loop(chips - 1, send_part)
    wait_rows(me_z)
    keep_rows.wait()
    own[...] = times_w(me_z)

    def add_part(i):
        z = lax.rem(me_z + i + 1, chips)
        part_arrival(z).wait_recv()

        @pl.loop(0, slots // block_rows)
        def _(j):
            at = pl.ds(pl.multiple_of(j * block_rows, block_rows), block_rows)
            own[at, :] += part_in[z, at, :].astype(F32)

    loop(chips - 1, add_part)

    keep_gate.wait()

    @pl.loop(1, ep)
    def _(k):
        gate_arrival(lax.rem(me_e + k, ep)).wait_recv()

    @pl.loop(0, ep)
    def _(e):
        at = pl.ds(pl.multiple_of(e * cap, cap), cap)
        score = jnp.sum(own[at, :] * hid[at, :].astype(F32), axis=1, keepdims=True)
        score_out[e] = jnp.broadcast_to(score, (cap, 128))

    @pl.loop(1, ep)
    def _(k):
        score_copy(lax.rem(me_e + k, ep)).start()

    keep_score.start()

    @pl.loop(0, ep)
    def _(e):
        at = pl.ds(pl.multiple_of(e * cap, cap), cap)
        scaled = own[at, :] * gate_in[e][:, :1]
        pre_v[at, :ff] = (scaled * fa[at, :]).astype(BF16)
        pre_v[at, ff:] = (scaled * fu[at, :]).astype(BF16)

    store = pltpu.make_async_copy(pre_v, pre_ref, load_sem.at[0])
    store.start()

    keep_score.wait()

    @pl.loop(1, ep)
    def _(k):
        score_arrival(lax.rem(me_e + k, ep)).wait_recv()

    got = score_in[...].reshape(slots, 128)
    spread = jnp.sum((chosen * got[:, :1]).reshape(ep, cap, tokens), axis=1)
    result = jnp.zeros((top, tokens), F32)
    for f in range(ep):
        result += jnp.where(routes == f * step, spread[f : f + 1, :], 0.0)
    gg_ref[...] = result

    def sent(k):
        e = lax.rem(me_e + k // chips, ep)
        z = lax.rem(me_z + k % chips, chips)
        row_copy(e, z).wait_send()

    @pl.loop(1, ep * chips)
    def _(k):
        sent(k)

    @pl.loop(1, ep)
    def _(k):
        e = lax.rem(me_e + k, ep)
        gate_copy(e).wait_send()
        score_copy(e).wait_send()

    @pl.loop(1, chips)
    def _(k):
        part_copy(lax.rem(me_z + k, chips)).wait_send()

    store.wait()


def on_device(ep, sp, grad_out, routes, gate, saved, w_down):
    tokens, width = grad_out.shape
    slots = saved.shape[2]
    ff = saved.shape[3] // 2
    kw = w_down.shape[2]
    cap = slots // ep
    chips = sp // 2
    cols = 2 * kw
    vmem = pl.BlockSpec(memory_space=pltpu.VMEM)
    hbm = pl.BlockSpec(memory_space=pl.ANY)
    pre, grad_gate = pl.pallas_call(
        functools.partial(kernel, ep, chips),
        out_shape=(
            jax.ShapeDtypeStruct((slots, 2 * ff), BF16),
            jax.ShapeDtypeStruct((routes.shape[1], tokens), F32),
        ),
        in_specs=[vmem, vmem, hbm, hbm, hbm],
        out_specs=(hbm, vmem),
        scratch_shapes=[
            pltpu.VMEM((tokens, width), BF16),
            pltpu.VMEM((slots, 2 * ff), BF16),
            pltpu.VMEM((2, ff, kw), BF16),
            pltpu.VMEM((chips, ep, cap, cols), BF16),
            pltpu.VMEM((chips, ep, cap, cols), BF16),
            pltpu.VMEM((ep, cap, 128), F32),
            pltpu.VMEM((ep, cap, 128), F32),
            pltpu.VMEM((chips, slots, ff), BF16),
            pltpu.VMEM((chips, slots, ff), BF16),
            pltpu.VMEM((ep, cap, 128), F32),
            pltpu.VMEM((ep, cap, 128), F32),
            pltpu.VMEM((slots, ff), F32),
            pltpu.VMEM((slots, ff), BF16),
            pltpu.VMEM((slots, ff), F32),
            pltpu.VMEM((slots, ff), F32),
            pltpu.VMEM((slots, 2 * ff), BF16),
            pltpu.SemaphoreType.DMA((3,)),
            pltpu.SemaphoreType.DMA((2,)),
            pltpu.SemaphoreType.DMA((2, chips, ep)),
            pltpu.SemaphoreType.DMA((2, ep)),
            pltpu.SemaphoreType.DMA((2, chips)),
            pltpu.SemaphoreType.DMA((2, ep)),
            pltpu.SemaphoreType.DMA((3,)),
        ],
        compiler_params=pltpu.CompilerParams(
            collective_id=0, has_side_effects=True, vmem_limit_bytes=56 * 1024 * 1024
        ),
    )(routes.T, gate.T, grad_out, saved.reshape(slots, 2 * ff), w_down.reshape(ff, kw))
    return pre.reshape(saved.shape), grad_gate.T


def solution(mesh):
    ep, sp = mesh.shape["ep"], mesh.shape["sp"]
    in_specs = (
        P(("ep", "sp"), None),
        P(("ep", "sp"), None),
        P(("ep", "sp"), None),
        P("ep", "sp", None, None),
        P("ep", None, "sp"),
    )
    out_specs = (P("ep", "sp", None, None), P(("ep", "sp"), None))
    return jax.shard_map(
        functools.partial(on_device, ep, sp),
        mesh=mesh,
        in_specs=in_specs,
        out_specs=out_specs,
        check_vma=False,
    )
```

```python
import functools

import jax
import jax.numpy as jnp
from jax import lax
from jax.experimental import pallas as pl
from jax.experimental.pallas import tpu as pltpu
from jax.sharding import PartitionSpec as P

EXPERTS = 128
MESH = pl.DeviceIdType.MESH
F32 = jnp.float32
BF16 = jnp.bfloat16


def loop(count, body):
    if count <= 4:
        for i in range(count):
            body(i)
    else:

        @pl.loop(0, count)
        def _(i):
            body(i)


def kernel(
    ep,
    chips,
    routes_ref,
    gate_ref,
    grad_ref,
    saved_ref,
    w_ref,
    pre_ref,
    gg_ref,
    grad_v,
    saved_v,
    wbuf,
    rows_out,
    rows_in,
    gate_out,
    gate_in,
    part_out,
    part_in,
    score_out,
    score_in,
    own,
    hid,
    fa,
    fu,
    pre_v,
    load_sem,
    w_sem,
    row_sem,
    gate_sem,
    part_sem,
    score_sem,
    local_sem,
):
    top, tokens = routes_ref.shape
    nt = (((1,), (1,)), ((), ()))
    relayed = chips == 4
    cap = rows_out.shape[2]
    cols = rows_out.shape[3]
    slots = ep * cap
    ff = w_ref.shape[0]
    kw = w_ref.shape[1]
    me_e = lax.axis_index("ep")
    me_s = lax.axis_index("sp")
    me_z = me_s // 2
    me_c = me_s % 2
    sibling = me_z * 2 + (1 - me_c)

    load_grad = pltpu.make_async_copy(grad_ref, grad_v, load_sem.at[0])
    load_grad.start()
    load_w = pltpu.make_async_copy(w_ref, wbuf.at[me_c], load_sem.at[1])
    load_w.start()
    load_saved = pltpu.make_async_copy(saved_ref, saved_v, load_sem.at[2])
    load_saved.start()

    barrier = pltpu.get_barrier_semaphore()
    pl.semaphore_signal(barrier, inc=1, device_id=(me_e, sibling), device_id_type=MESH)

    def greet(k):
        e = lax.rem(me_e + k // chips, ep)
        z = lax.rem(me_z + k % chips, chips)
        pl.semaphore_signal(barrier, inc=1, device_id=(e, z * 2 + me_c), device_id_type=MESH)

    @pl.loop(1, ep * chips)
    def _(k):
        greet(k)

    step = EXPERTS // ep
    routes = routes_ref[...]
    gates = gate_ref[...].astype(F32)
    slot_id = lax.broadcasted_iota(jnp.int32, (slots, tokens), 0)
    place_id = (slot_id % cap).astype(F32)
    members, weights = [], []
    for f in range(ep):
        hit = (routes == f * step).astype(F32)
        count = jnp.sum(hit, axis=0, keepdims=True)
        value = jnp.sum(hit * gates, axis=0, keepdims=True)
        members.append(jnp.broadcast_to(count, (cap, tokens)))
        weights.append(jnp.broadcast_to(value, (cap, tokens)))
    member = jnp.concatenate(members, axis=0)
    weight = jnp.concatenate(weights, axis=0)
    before = (
        lax.broadcasted_iota(jnp.int32, (tokens, tokens), 0)
        < lax.broadcasted_iota(jnp.int32, (tokens, tokens), 1)
    ).astype(F32)
    place = jnp.dot(member.astype(BF16), before.astype(BF16), preferred_element_type=F32)
    chosen = jnp.where((place == place_id) & (member > 0.5), 1.0, 0.0)
    picked = jnp.sum(chosen * weight, axis=1, keepdims=True)
    gate_out[...] = jnp.broadcast_to(picked, (slots, 128)).reshape(ep, cap, 128)
    chosen16 = chosen.astype(BF16)

    load_grad.wait()
    pl.semaphore_wait(barrier, ep * chips)

    w_copy = pltpu.make_async_remote_copy(
        src_ref=w_ref,
        dst_ref=wbuf.at[me_c],
        send_sem=w_sem.at[0],
        recv_sem=w_sem.at[1],
        device_id=(me_e, sibling),
        device_id_type=MESH,
    )
    w_copy.start()

    def row_copy(e, z):
        return pltpu.make_async_remote_copy(
            src_ref=rows_out.at[z, e],
            dst_ref=rows_in.at[me_z, me_e],
            send_sem=row_sem.at[0, z, e],
            recv_sem=row_sem.at[1, me_z, me_e],
            device_id=(e, z * 2 + me_c),
            device_id_type=MESH,
        )

    def row_arrival(e, z):
        return pltpu.make_async_remote_copy(
            src_ref=rows_out.at[me_z, me_e],
            dst_ref=rows_in.at[z, e],
            send_sem=row_sem.at[0, me_z, me_e],
            recv_sem=row_sem.at[1, z, e],
            device_id=(e, z * 2 + me_c),
            device_id_type=MESH,
        )

    def gate_copy(e):
        return pltpu.make_async_remote_copy(
            src_ref=gate_out.at[e],
            dst_ref=gate_in.at[me_e],
            send_sem=gate_sem.at[0, e],
            recv_sem=gate_sem.at[1, me_e],
            device_id=(e, me_s),
            device_id_type=MESH,
        )

    def gate_arrival(e):
        return pltpu.make_async_remote_copy(
            src_ref=gate_out.at[me_e],
            dst_ref=gate_in.at[e],
            send_sem=gate_sem.at[0, me_e],
            recv_sem=gate_sem.at[1, e],
            device_id=(e, me_s),
            device_id_type=MESH,
        )

    def score_copy(e):
        return pltpu.make_async_remote_copy(
            src_ref=score_out.at[e],
            dst_ref=score_in.at[me_e],
            send_sem=score_sem.at[0, e],
            recv_sem=score_sem.at[1, me_e],
            device_id=(e, me_s),
            device_id_type=MESH,
        )

    def score_arrival(e):
        return pltpu.make_async_remote_copy(
            src_ref=score_out.at[me_e],
            dst_ref=score_in.at[e],
            send_sem=score_sem.at[0, me_e],
            recv_sem=score_sem.at[1, e],
            device_id=(e, me_s),
            device_id_type=MESH,
        )

    def part_copy(z):
        return pltpu.make_async_remote_copy(
            src_ref=part_out.at[z],
            dst_ref=part_in.at[me_z],
            send_sem=part_sem.at[0, z, 0],
            recv_sem=part_sem.at[1, me_z, 0],
            device_id=(me_e, z * 2 + me_c),
            device_id_type=MESH,
        )

    def part_arrival(z):
        return pltpu.make_async_remote_copy(
            src_ref=part_out.at[me_z],
            dst_ref=part_in.at[z],
            send_sem=part_sem.at[0, me_z, 0],
            recv_sem=part_sem.at[1, z, 0],
            device_id=(me_e, z * 2 + me_c),
            device_id_type=MESH,
        )

    keep_rows = pltpu.make_async_copy(
        rows_out.at[me_z, me_e], rows_in.at[me_z, me_e], local_sem.at[0]
    )
    keep_gate = pltpu.make_async_copy(gate_out.at[me_e], gate_in.at[me_e], local_sem.at[1])
    keep_score = pltpu.make_async_copy(score_out.at[me_e], score_in.at[me_e], local_sem.at[2])

    half = me_z // 2
    partner = me_z + 1 - 2 * (me_z % 2)
    across = [3 * (1 - half), 2 - half]

    def send_rows(i):
        if relayed:
            z = [*across, partner, me_z][i]
        else:
            z = lax.rem(me_z + i + 1, chips)
        block = jnp.dot(
            chosen16,
            grad_v[:, pl.ds(pl.multiple_of(z * cols, cols), cols)],
            preferred_element_type=F32,
        )
        rows_out[z] = block.astype(BF16).reshape(ep, cap, cols)

        def one(k):
            e = lax.rem(me_e + k, ep)

            @pl.when((e != me_e) | (z != me_z))
            def _():
                row_copy(e, z).start()

        loop(ep, one)

    loop(chips, send_rows)
    keep_rows.start()
    keep_gate.start()

    @pl.loop(1, ep)
    def _(k):
        gate_copy(lax.rem(me_e + k, ep)).start()

    load_saved.wait()
    block_rows = 16

    @pl.loop(0, slots // block_rows)
    def _(i):
        at = pl.ds(pl.multiple_of(i * block_rows, block_rows), block_rows)
        a = saved_v[at, :ff].astype(F32)
        u = saved_v[at, ff:].astype(F32)
        sig = jax.nn.sigmoid(a)
        silu = a * sig
        hid[at, :] = (silu * u).astype(BF16)
        fa[at, :] = u * sig * (1.0 + a * (1.0 - sig))
        fu[at, :] = silu

    load_w.wait()
    w_copy.wait()

    def times_w(z):
        rows = rows_in[z].reshape(slots, cols)
        return lax.dot_general(
            rows[:, :kw], wbuf[0], nt, preferred_element_type=F32
        ) + lax.dot_general(rows[:, kw:], wbuf[1], nt, preferred_element_type=F32)

    def wait_rows(z):
        def one(k):
            e = lax.rem(me_e + k, ep)

            @pl.when((e != me_e) | (z != me_z))
            def _():
                row_arrival(e, z).wait_recv()

        loop(ep, one)

    piece = slots // 2

    def post(i, j, c, z):
        at = pl.ds(c * piece, piece)
        return pltpu.make_async_remote_copy(
            src_ref=part_out.at[i, at],
            dst_ref=part_in.at[j, at],
            send_sem=part_sem.at[0, i, c],
            recv_sem=part_sem.at[1, j, c],
            device_id=(me_e, z * 2 + me_c),
            device_id_type=MESH,
        )

    def relay_parts():
        edge = me_z % 3 == 0
        for i in range(2):
            wait_rows(across[i])
            own[...] = times_w(across[i])
            for c in range(2):
                at = pl.ds(c * piece, piece)

                @pl.when(edge)
                def _():
                    part_out[i, at, :] = own[at, :].astype(BF16)
                    post(i, 2 + i, c, partner).start()

                @pl.when(jnp.logical_not(edge))
                def _():
                    post(i, 2 + i, c, partner).wait_recv()
                    total = own[at, :] + part_in[2 + i, at, :].astype(F32)
                    part_out[i, at, :] = total.astype(BF16)
                    post(i, 1, c, across[i]).start()

        wait_rows(partner)
        part_out[2] = times_w(partner).astype(BF16)
        for c in range(2):
            post(2, 0, c, partner).start()
        wait_rows(me_z)
        keep_rows.wait()
        own[...] = times_w(me_z)
        for j in range(2):
            for c in range(2):
                at = pl.ds(c * piece, piece)
                post(2, j, c, partner).wait_recv()
                own[at, :] += part_in[j, at, :].astype(F32)

    if relayed:
        relay_parts()
    else:
        def send_part(i):
            z = lax.rem(me_z + chips - 1 - i, chips)
            wait_rows(z)
            part_out[z] = times_w(z).astype(BF16)
            part_copy(z).start()

        loop(chips - 1, send_part)
        wait_rows(me_z)
        keep_rows.wait()
        own[...] = times_w(me_z)

        def add_part(i):
            z = lax.rem(me_z + i + 1, chips)
            part_arrival(z).wait_recv()

            @pl.loop(0, slots // block_rows)
            def _(j):
                at = pl.ds(pl.multiple_of(j * block_rows, block_rows), block_rows)
                own[at, :] += part_in[z, at, :].astype(F32)

        loop(chips - 1, add_part)

    keep_gate.wait()

    @pl.loop(1, ep)
    def _(k):
        gate_arrival(lax.rem(me_e + k, ep)).wait_recv()

    @pl.loop(0, ep)
    def _(e):
        at = pl.ds(pl.multiple_of(e * cap, cap), cap)
        score = jnp.sum(own[at, :] * hid[at, :].astype(F32), axis=1, keepdims=True)
        score_out[e] = jnp.broadcast_to(score, (cap, 128))

    @pl.loop(1, ep)
    def _(k):
        score_copy(lax.rem(me_e + k, ep)).start()

    keep_score.start()

    @pl.loop(0, ep)
    def _(e):
        at = pl.ds(pl.multiple_of(e * cap, cap), cap)
        scaled = own[at, :] * gate_in[e][:, :1]
        pre_v[at, :ff] = (scaled * fa[at, :]).astype(BF16)
        pre_v[at, ff:] = (scaled * fu[at, :]).astype(BF16)

    store = pltpu.make_async_copy(pre_v, pre_ref, load_sem.at[0])
    store.start()

    keep_score.wait()

    @pl.loop(1, ep)
    def _(k):
        score_arrival(lax.rem(me_e + k, ep)).wait_recv()

    got = score_in[...].reshape(slots, 128)
    spread = jnp.sum((chosen * got[:, :1]).reshape(ep, cap, tokens), axis=1)
    result = jnp.zeros((top, tokens), F32)
    for f in range(ep):
        result += jnp.where(routes == f * step, spread[f : f + 1, :], 0.0)
    gg_ref[...] = result

    def sent(k):
        e = lax.rem(me_e + k // chips, ep)
        z = lax.rem(me_z + k % chips, chips)
        row_copy(e, z).wait_send()

    @pl.loop(1, ep * chips)
    def _(k):
        sent(k)

    @pl.loop(1, ep)
    def _(k):
        e = lax.rem(me_e + k, ep)
        gate_copy(e).wait_send()
        score_copy(e).wait_send()

    if relayed:
        for i in range(3):
            for c in range(2):
                post(i, 0, c, partner).wait_send()
    else:

        @pl.loop(1, chips)
        def _(k):
            part_copy(lax.rem(me_z + k, chips)).wait_send()

    store.wait()


def on_device(ep, sp, grad_out, routes, gate, saved, w_down):
    tokens, width = grad_out.shape
    slots = saved.shape[2]
    ff = saved.shape[3] // 2
    kw = w_down.shape[2]
    cap = slots // ep
    chips = sp // 2
    cols = 2 * kw
    vmem = pl.BlockSpec(memory_space=pltpu.VMEM)
    hbm = pl.BlockSpec(memory_space=pl.ANY)
    pre, grad_gate = pl.pallas_call(
        functools.partial(kernel, ep, chips),
        out_shape=(
            jax.ShapeDtypeStruct((slots, 2 * ff), BF16),
            jax.ShapeDtypeStruct((routes.shape[1], tokens), F32),
        ),
        in_specs=[vmem, vmem, hbm, hbm, hbm],
        out_specs=(hbm, vmem),
        scratch_shapes=[
            pltpu.VMEM((tokens, width), BF16),
            pltpu.VMEM((slots, 2 * ff), BF16),
            pltpu.VMEM((2, ff, kw), BF16),
            pltpu.VMEM((chips, ep, cap, cols), BF16),
            pltpu.VMEM((chips, ep, cap, cols), BF16),
            pltpu.VMEM((ep, cap, 128), F32),
            pltpu.VMEM((ep, cap, 128), F32),
            pltpu.VMEM((chips, slots, ff), BF16),
            pltpu.VMEM((chips, slots, ff), BF16),
            pltpu.VMEM((ep, cap, 128), F32),
            pltpu.VMEM((ep, cap, 128), F32),
            pltpu.VMEM((slots, ff), F32),
            pltpu.VMEM((slots, ff), BF16),
            pltpu.VMEM((slots, ff), F32),
            pltpu.VMEM((slots, ff), F32),
            pltpu.VMEM((slots, 2 * ff), BF16),
            pltpu.SemaphoreType.DMA((3,)),
            pltpu.SemaphoreType.DMA((2,)),
            pltpu.SemaphoreType.DMA((2, chips, ep)),
            pltpu.SemaphoreType.DMA((2, ep)),
            pltpu.SemaphoreType.DMA((2, chips, 2)),
            pltpu.SemaphoreType.DMA((2, ep)),
            pltpu.SemaphoreType.DMA((3,)),
        ],
        compiler_params=pltpu.CompilerParams(
            collective_id=0, has_side_effects=True, vmem_limit_bytes=56 * 1024 * 1024
        ),
    )(routes.T, gate.T, grad_out, saved.reshape(slots, 2 * ff), w_down.reshape(ff, kw))
    return pre.reshape(saved.shape), grad_gate.T


def solution(mesh):
    ep, sp = mesh.shape["ep"], mesh.shape["sp"]
    in_specs = (
        P(("ep", "sp"), None),
        P(("ep", "sp"), None),
        P(("ep", "sp"), None),
        P("ep", "sp", None, None),
        P("ep", None, "sp"),
    )
    out_specs = (P("ep", "sp", None, None), P(("ep", "sp"), None))
    return jax.shard_map(
        functools.partial(on_device, ep, sp),
        mesh=mesh,
        in_specs=in_specs,
        out_specs=out_specs,
        check_vma=False,
    )
```

```python
import functools

import jax
import jax.numpy as jnp
from jax import lax
from jax.experimental import pallas as pl
from jax.experimental.pallas import tpu as pltpu
from jax.sharding import PartitionSpec as P

EXPERTS = 128
MESH = pl.DeviceIdType.MESH
F32 = jnp.float32
BF16 = jnp.bfloat16


def loop(count, body):
    if count <= 4:
        for i in range(count):
            body(i)
    else:

        @pl.loop(0, count)
        def _(i):
            body(i)


def kernel(
    ep,
    chips,
    routes_ref,
    gate_ref,
    grad_ref,
    saved_ref,
    w_ref,
    pre_ref,
    gg_ref,
    grad_v,
    saved_v,
    wbuf,
    rows_out,
    rows_in,
    gate_out,
    gate_in,
    part_out,
    part_in,
    score_out,
    score_in,
    own,
    hid,
    fa,
    fu,
    pre_v,
    load_sem,
    w_sem,
    row_sem,
    gate_sem,
    part_sem,
    score_sem,
    local_sem,
):
    top, tokens = routes_ref.shape
    nt = (((1,), (1,)), ((), ()))
    relayed = chips == 4
    cap = rows_out.shape[2]
    cols = rows_out.shape[3]
    slots = ep * cap
    ff = w_ref.shape[0]
    kw = w_ref.shape[1]
    me_e = lax.axis_index("ep")
    me_s = lax.axis_index("sp")
    me_z = me_s // 2
    me_c = me_s % 2
    sibling = me_z * 2 + (1 - me_c)

    load_grad = pltpu.make_async_copy(grad_ref, grad_v, load_sem.at[0])
    load_grad.start()
    load_w = pltpu.make_async_copy(w_ref, wbuf.at[me_c], load_sem.at[1])
    load_w.start()
    load_saved = pltpu.make_async_copy(saved_ref, saved_v, load_sem.at[2])
    load_saved.start()

    barrier = pltpu.get_barrier_semaphore()
    pl.semaphore_signal(barrier, inc=1, device_id=(me_e, sibling), device_id_type=MESH)

    def greet(k):
        e = lax.rem(me_e + k // chips, ep)
        z = lax.rem(me_z + k % chips, chips)
        pl.semaphore_signal(barrier, inc=1, device_id=(e, z * 2 + me_c), device_id_type=MESH)

    @pl.loop(1, ep * chips)
    def _(k):
        greet(k)

    step = EXPERTS // ep
    routes = routes_ref[...]
    gates = gate_ref[...].astype(F32)
    slot_id = lax.broadcasted_iota(jnp.int32, (slots, tokens), 0)
    place_id = (slot_id % cap).astype(F32)
    members, weights = [], []
    for f in range(ep):
        hit = (routes == f * step).astype(F32)
        count = jnp.sum(hit, axis=0, keepdims=True)
        value = jnp.sum(hit * gates, axis=0, keepdims=True)
        members.append(jnp.broadcast_to(count, (cap, tokens)))
        weights.append(jnp.broadcast_to(value, (cap, tokens)))
    member = jnp.concatenate(members, axis=0)
    weight = jnp.concatenate(weights, axis=0)
    before = (
        lax.broadcasted_iota(jnp.int32, (tokens, tokens), 0)
        < lax.broadcasted_iota(jnp.int32, (tokens, tokens), 1)
    ).astype(F32)
    place = jnp.dot(member.astype(BF16), before.astype(BF16), preferred_element_type=F32)
    chosen = jnp.where((place == place_id) & (member > 0.5), 1.0, 0.0)
    picked = jnp.sum(chosen * weight, axis=1, keepdims=True)
    gate_out[...] = jnp.broadcast_to(picked, (slots, 128)).reshape(ep, cap, 128)
    chosen16 = chosen.astype(BF16)

    load_grad.wait()
    pl.semaphore_wait(barrier, ep * chips)

    w_copy = pltpu.make_async_remote_copy(
        src_ref=w_ref,
        dst_ref=wbuf.at[me_c],
        send_sem=w_sem.at[0],
        recv_sem=w_sem.at[1],
        device_id=(me_e, sibling),
        device_id_type=MESH,
    )

    def row_copy(e, z):
        return pltpu.make_async_remote_copy(
            src_ref=rows_out.at[z, e],
            dst_ref=rows_in.at[me_z, me_e],
            send_sem=row_sem.at[0, z, e],
            recv_sem=row_sem.at[1, me_z, me_e],
            device_id=(e, z * 2 + me_c),
            device_id_type=MESH,
        )

    def row_arrival(e, z):
        return pltpu.make_async_remote_copy(
            src_ref=rows_out.at[me_z, me_e],
            dst_ref=rows_in.at[z, e],
            send_sem=row_sem.at[0, me_z, me_e],
            recv_sem=row_sem.at[1, z, e],
            device_id=(e, z * 2 + me_c),
            device_id_type=MESH,
        )

    def gate_copy(e):
        return pltpu.make_async_remote_copy(
            src_ref=gate_out.at[e],
            dst_ref=gate_in.at[me_e],
            send_sem=gate_sem.at[0, e],
            recv_sem=gate_sem.at[1, me_e],
            device_id=(e, me_s),
            device_id_type=MESH,
        )

    def gate_arrival(e):
        return pltpu.make_async_remote_copy(
            src_ref=gate_out.at[me_e],
            dst_ref=gate_in.at[e],
            send_sem=gate_sem.at[0, me_e],
            recv_sem=gate_sem.at[1, e],
            device_id=(e, me_s),
            device_id_type=MESH,
        )

    def score_copy(e):
        return pltpu.make_async_remote_copy(
            src_ref=score_out.at[e],
            dst_ref=score_in.at[me_e],
            send_sem=score_sem.at[0, e],
            recv_sem=score_sem.at[1, me_e],
            device_id=(e, me_s),
            device_id_type=MESH,
        )

    def score_arrival(e):
        return pltpu.make_async_remote_copy(
            src_ref=score_out.at[me_e],
            dst_ref=score_in.at[e],
            send_sem=score_sem.at[0, me_e],
            recv_sem=score_sem.at[1, e],
            device_id=(e, me_s),
            device_id_type=MESH,
        )

    def part_copy(z):
        return pltpu.make_async_remote_copy(
            src_ref=part_out.at[z],
            dst_ref=part_in.at[me_z],
            send_sem=part_sem.at[0, z, 0],
            recv_sem=part_sem.at[1, me_z, 0],
            device_id=(me_e, z * 2 + me_c),
            device_id_type=MESH,
        )

    def part_arrival(z):
        return pltpu.make_async_remote_copy(
            src_ref=part_out.at[me_z],
            dst_ref=part_in.at[z],
            send_sem=part_sem.at[0, me_z, 0],
            recv_sem=part_sem.at[1, z, 0],
            device_id=(me_e, z * 2 + me_c),
            device_id_type=MESH,
        )

    keep_rows = pltpu.make_async_copy(
        rows_out.at[me_z, me_e], rows_in.at[me_z, me_e], local_sem.at[0]
    )
    keep_gate = pltpu.make_async_copy(gate_out.at[me_e], gate_in.at[me_e], local_sem.at[1])
    keep_score = pltpu.make_async_copy(score_out.at[me_e], score_in.at[me_e], local_sem.at[2])

    half = me_z // 2
    partner = me_z + 1 - 2 * (me_z % 2)
    across = [3 * (1 - half), 2 - half]

    def send_rows(i):
        if relayed:
            z = [*across, partner, me_z][i]
        else:
            z = lax.rem(me_z + i + 1, chips)
        block = jnp.dot(
            chosen16,
            grad_v[:, pl.ds(pl.multiple_of(z * cols, cols), cols)],
            preferred_element_type=F32,
        )
        rows_out[z] = block.astype(BF16).reshape(ep, cap, cols)

        def one(k):
            e = lax.rem(me_e + k, ep)

            @pl.when((e != me_e) | (z != me_z))
            def _():
                row_copy(e, z).start()

        loop(ep, one)

    loop(chips, send_rows)
    w_copy.start()
    keep_rows.start()
    keep_gate.start()

    @pl.loop(1, ep)
    def _(k):
        gate_copy(lax.rem(me_e + k, ep)).start()

    load_saved.wait()
    block_rows = 16

    @pl.loop(0, slots // block_rows)
    def _(i):
        at = pl.ds(pl.multiple_of(i * block_rows, block_rows), block_rows)
        a = saved_v[at, :ff].astype(F32)
        u = saved_v[at, ff:].astype(F32)
        sig = jax.nn.sigmoid(a)
        silu = a * sig
        hid[at, :] = (silu * u).astype(BF16)
        fa[at, :] = u * sig * (1.0 + a * (1.0 - sig))
        fu[at, :] = silu

    load_w.wait()
    w_copy.wait()

    def times_w(z):
        rows = rows_in[z].reshape(slots, cols)
        return lax.dot_general(
            rows[:, :kw], wbuf[0], nt, preferred_element_type=F32
        ) + lax.dot_general(rows[:, kw:], wbuf[1], nt, preferred_element_type=F32)

    def wait_rows(z):
        def one(k):
            e = lax.rem(me_e + k, ep)

            @pl.when((e != me_e) | (z != me_z))
            def _():
                row_arrival(e, z).wait_recv()

        loop(ep, one)

    piece = slots // 4

    def post(i, j, c, z):
        at = pl.ds(c * piece, piece)
        return pltpu.make_async_remote_copy(
            src_ref=part_out.at[i, at],
            dst_ref=part_in.at[j, at],
            send_sem=part_sem.at[0, i, c],
            recv_sem=part_sem.at[1, j, c],
            device_id=(me_e, z * 2 + me_c),
            device_id_type=MESH,
        )

    def relay_parts():
        edge = me_z % 3 == 0

        def send_partner():
            wait_rows(partner)
            part_out[2] = times_w(partner).astype(BF16)
            for c in range(4):
                post(2, 0, c, partner).start()

        pl.when(jnp.logical_not(edge))(send_partner)
        for i in range(2):
            wait_rows(across[i])
            own[...] = times_w(across[i])
            for c in range(4):
                at = pl.ds(c * piece, piece)

                @pl.when(edge)
                def _():
                    part_out[i, at, :] = own[at, :].astype(BF16)
                    post(i, 2 + i, c, partner).start()

                @pl.when(jnp.logical_not(edge))
                def _():
                    post(i, 2 + i, c, partner).wait_recv()
                    total = own[at, :] + part_in[2 + i, at, :].astype(F32)
                    part_out[i, at, :] = total.astype(BF16)
                    post(i, 1, c, across[i]).start()

        pl.when(edge)(send_partner)
        wait_rows(me_z)
        keep_rows.wait()
        own[...] = times_w(me_z)
        for j in range(2):
            for c in range(4):
                at = pl.ds(c * piece, piece)
                post(2, j, c, partner).wait_recv()
                own[at, :] += part_in[j, at, :].astype(F32)

    if relayed:
        relay_parts()
    else:
        def send_part(i):
            z = lax.rem(me_z + chips - 1 - i, chips)
            wait_rows(z)
            part_out[z] = times_w(z).astype(BF16)
            part_copy(z).start()

        loop(chips - 1, send_part)
        wait_rows(me_z)
        keep_rows.wait()
        own[...] = times_w(me_z)

        def add_part(i):
            z = lax.rem(me_z + i + 1, chips)
            part_arrival(z).wait_recv()

            @pl.loop(0, slots // block_rows)
            def _(j):
                at = pl.ds(pl.multiple_of(j * block_rows, block_rows), block_rows)
                own[at, :] += part_in[z, at, :].astype(F32)

        loop(chips - 1, add_part)

    keep_gate.wait()

    @pl.loop(1, ep)
    def _(k):
        gate_arrival(lax.rem(me_e + k, ep)).wait_recv()

    @pl.loop(0, ep)
    def _(e):
        at = pl.ds(pl.multiple_of(e * cap, cap), cap)
        score = jnp.sum(own[at, :] * hid[at, :].astype(F32), axis=1, keepdims=True)
        score_out[e] = jnp.broadcast_to(score, (cap, 128))

    @pl.loop(1, ep)
    def _(k):
        score_copy(lax.rem(me_e + k, ep)).start()

    keep_score.start()

    @pl.loop(0, ep)
    def _(e):
        at = pl.ds(pl.multiple_of(e * cap, cap), cap)
        scaled = own[at, :] * gate_in[e][:, :1]
        pre_v[at, :ff] = (scaled * fa[at, :]).astype(BF16)
        pre_v[at, ff:] = (scaled * fu[at, :]).astype(BF16)

    store = pltpu.make_async_copy(pre_v, pre_ref, load_sem.at[0])
    store.start()

    keep_score.wait()

    @pl.loop(1, ep)
    def _(k):
        score_arrival(lax.rem(me_e + k, ep)).wait_recv()

    got = score_in[...].reshape(slots, 128)
    spread = jnp.sum((chosen * got[:, :1]).reshape(ep, cap, tokens), axis=1)
    result = jnp.zeros((top, tokens), F32)
    for f in range(ep):
        result += jnp.where(routes == f * step, spread[f : f + 1, :], 0.0)
    gg_ref[...] = result

    def sent(k):
        e = lax.rem(me_e + k // chips, ep)
        z = lax.rem(me_z + k % chips, chips)
        row_copy(e, z).wait_send()

    @pl.loop(1, ep * chips)
    def _(k):
        sent(k)

    @pl.loop(1, ep)
    def _(k):
        e = lax.rem(me_e + k, ep)
        gate_copy(e).wait_send()
        score_copy(e).wait_send()

    if relayed:
        for i in range(3):
            for c in range(4):
                post(i, 0, c, partner).wait_send()
    else:

        @pl.loop(1, chips)
        def _(k):
            part_copy(lax.rem(me_z + k, chips)).wait_send()

    store.wait()


def on_device(ep, sp, grad_out, routes, gate, saved, w_down):
    tokens, width = grad_out.shape
    slots = saved.shape[2]
    ff = saved.shape[3] // 2
    kw = w_down.shape[2]
    cap = slots // ep
    chips = sp // 2
    cols = 2 * kw
    vmem = pl.BlockSpec(memory_space=pltpu.VMEM)
    hbm = pl.BlockSpec(memory_space=pl.ANY)
    pre, grad_gate = pl.pallas_call(
        functools.partial(kernel, ep, chips),
        out_shape=(
            jax.ShapeDtypeStruct((slots, 2 * ff), BF16),
            jax.ShapeDtypeStruct((routes.shape[1], tokens), F32),
        ),
        in_specs=[vmem, vmem, hbm, hbm, hbm],
        out_specs=(hbm, vmem),
        scratch_shapes=[
            pltpu.VMEM((tokens, width), BF16),
            pltpu.VMEM((slots, 2 * ff), BF16),
            pltpu.VMEM((2, ff, kw), BF16),
            pltpu.VMEM((chips, ep, cap, cols), BF16),
            pltpu.VMEM((chips, ep, cap, cols), BF16),
            pltpu.VMEM((ep, cap, 128), F32),
            pltpu.VMEM((ep, cap, 128), F32),
            pltpu.VMEM((chips, slots, ff), BF16),
            pltpu.VMEM((chips, slots, ff), BF16),
            pltpu.VMEM((ep, cap, 128), F32),
            pltpu.VMEM((ep, cap, 128), F32),
            pltpu.VMEM((slots, ff), F32),
            pltpu.VMEM((slots, ff), BF16),
            pltpu.VMEM((slots, ff), F32),
            pltpu.VMEM((slots, ff), F32),
            pltpu.VMEM((slots, 2 * ff), BF16),
            pltpu.SemaphoreType.DMA((3,)),
            pltpu.SemaphoreType.DMA((2,)),
            pltpu.SemaphoreType.DMA((2, chips, ep)),
            pltpu.SemaphoreType.DMA((2, ep)),
            pltpu.SemaphoreType.DMA((2, chips, 4)),
            pltpu.SemaphoreType.DMA((2, ep)),
            pltpu.SemaphoreType.DMA((3,)),
        ],
        compiler_params=pltpu.CompilerParams(
            collective_id=0, has_side_effects=True, vmem_limit_bytes=56 * 1024 * 1024
        ),
    )(routes.T, gate.T, grad_out, saved.reshape(slots, 2 * ff), w_down.reshape(ff, kw))
    return pre.reshape(saved.shape), grad_gate.T


def solution(mesh):
    ep, sp = mesh.shape["ep"], mesh.shape["sp"]
    in_specs = (
        P(("ep", "sp"), None),
        P(("ep", "sp"), None),
        P(("ep", "sp"), None),
        P("ep", "sp", None, None),
        P("ep", None, "sp"),
    )
    out_specs = (P("ep", "sp", None, None), P(("ep", "sp"), None))
    return jax.shard_map(
        functools.partial(on_device, ep, sp),
        mesh=mesh,
        in_specs=in_specs,
        out_specs=out_specs,
        check_vma=False,
    )
```

```python
import functools

import jax
import jax.numpy as jnp
from jax import lax
from jax.experimental import pallas as pl
from jax.experimental.pallas import tpu as pltpu
from jax.sharding import PartitionSpec as P

EXPERTS = 128
MESH = pl.DeviceIdType.MESH
F32 = jnp.float32
BF16 = jnp.bfloat16


def loop(count, body):
    if count <= 4:
        for i in range(count):
            body(i)
    else:

        @pl.loop(0, count)
        def _(i):
            body(i)


def kernel(
    ep,
    chips,
    routes_ref,
    gate_ref,
    grad_ref,
    saved_ref,
    w_ref,
    pre_ref,
    gg_ref,
    grad_v,
    saved_v,
    wbuf,
    rows_out,
    rows_in,
    gate_out,
    gate_in,
    part_out,
    part_in,
    score_out,
    score_in,
    own,
    tmp,
    hid,
    fa,
    fu,
    pre_v,
    load_sem,
    w_sem,
    row_sem,
    gate_sem,
    part_sem,
    score_sem,
    local_sem,
):
    top, tokens = routes_ref.shape
    nt = (((1,), (1,)), ((), ()))
    relayed = chips == 4
    cap = rows_out.shape[2]
    cols = rows_out.shape[3]
    slots = ep * cap
    ff = w_ref.shape[0]
    kw = w_ref.shape[1]
    me_e = lax.axis_index("ep")
    me_s = lax.axis_index("sp")
    me_z = me_s // 2
    me_c = me_s % 2
    sibling = me_z * 2 + (1 - me_c)

    load_grad = pltpu.make_async_copy(grad_ref, grad_v, load_sem.at[0])
    load_grad.start()
    load_w = pltpu.make_async_copy(w_ref, wbuf.at[me_c], load_sem.at[1])
    load_w.start()
    load_saved = pltpu.make_async_copy(saved_ref, saved_v, load_sem.at[2])
    load_saved.start()

    barrier = pltpu.get_barrier_semaphore()
    pl.semaphore_signal(barrier, inc=1, device_id=(me_e, sibling), device_id_type=MESH)

    def greet(k):
        e = lax.rem(me_e + k // chips, ep)
        z = lax.rem(me_z + k % chips, chips)
        pl.semaphore_signal(barrier, inc=1, device_id=(e, z * 2 + me_c), device_id_type=MESH)

    @pl.loop(1, ep * chips)
    def _(k):
        greet(k)

    step = EXPERTS // ep
    routes = routes_ref[...]
    gates = gate_ref[...].astype(F32)
    slot_id = lax.broadcasted_iota(jnp.int32, (slots, tokens), 0)
    place_id = (slot_id % cap).astype(F32)
    members, weights = [], []
    for f in range(ep):
        hit = (routes == f * step).astype(F32)
        count = jnp.sum(hit, axis=0, keepdims=True)
        value = jnp.sum(hit * gates, axis=0, keepdims=True)
        members.append(jnp.broadcast_to(count, (cap, tokens)))
        weights.append(jnp.broadcast_to(value, (cap, tokens)))
    member = jnp.concatenate(members, axis=0)
    weight = jnp.concatenate(weights, axis=0)
    before = (
        lax.broadcasted_iota(jnp.int32, (tokens, tokens), 0)
        < lax.broadcasted_iota(jnp.int32, (tokens, tokens), 1)
    ).astype(F32)
    place = jnp.dot(member.astype(BF16), before.astype(BF16), preferred_element_type=F32)
    chosen = jnp.where((place == place_id) & (member > 0.5), 1.0, 0.0)
    picked = jnp.sum(chosen * weight, axis=1, keepdims=True)
    gate_out[...] = jnp.broadcast_to(picked, (slots, 128)).reshape(ep, cap, 128)
    chosen16 = chosen.astype(BF16)

    load_grad.wait()
    pl.semaphore_wait(barrier, ep * chips)

    w_copy = pltpu.make_async_remote_copy(
        src_ref=w_ref,
        dst_ref=wbuf.at[me_c],
        send_sem=w_sem.at[0],
        recv_sem=w_sem.at[1],
        device_id=(me_e, sibling),
        device_id_type=MESH,
    )

    def row_copy(e, z):
        return pltpu.make_async_remote_copy(
            src_ref=rows_out.at[z, e],
            dst_ref=rows_in.at[me_z, me_e],
            send_sem=row_sem.at[0, z, e],
            recv_sem=row_sem.at[1, me_z, me_e],
            device_id=(e, z * 2 + me_c),
            device_id_type=MESH,
        )

    def row_arrival(e, z):
        return pltpu.make_async_remote_copy(
            src_ref=rows_out.at[me_z, me_e],
            dst_ref=rows_in.at[z, e],
            send_sem=row_sem.at[0, me_z, me_e],
            recv_sem=row_sem.at[1, z, e],
            device_id=(e, z * 2 + me_c),
            device_id_type=MESH,
        )

    def gate_copy(e):
        return pltpu.make_async_remote_copy(
            src_ref=gate_out.at[e],
            dst_ref=gate_in.at[me_e],
            send_sem=gate_sem.at[0, e],
            recv_sem=gate_sem.at[1, me_e],
            device_id=(e, me_s),
            device_id_type=MESH,
        )

    def gate_arrival(e):
        return pltpu.make_async_remote_copy(
            src_ref=gate_out.at[me_e],
            dst_ref=gate_in.at[e],
            send_sem=gate_sem.at[0, me_e],
            recv_sem=gate_sem.at[1, e],
            device_id=(e, me_s),
            device_id_type=MESH,
        )

    def score_copy(e):
        return pltpu.make_async_remote_copy(
            src_ref=score_out.at[e],
            dst_ref=score_in.at[me_e],
            send_sem=score_sem.at[0, e],
            recv_sem=score_sem.at[1, me_e],
            device_id=(e, me_s),
            device_id_type=MESH,
        )

    def score_arrival(e):
        return pltpu.make_async_remote_copy(
            src_ref=score_out.at[me_e],
            dst_ref=score_in.at[e],
            send_sem=score_sem.at[0, me_e],
            recv_sem=score_sem.at[1, e],
            device_id=(e, me_s),
            device_id_type=MESH,
        )

    def part_copy(z):
        return pltpu.make_async_remote_copy(
            src_ref=part_out.at[z],
            dst_ref=part_in.at[me_z],
            send_sem=part_sem.at[0, z, 0],
            recv_sem=part_sem.at[1, me_z, 0],
            device_id=(me_e, z * 2 + me_c),
            device_id_type=MESH,
        )

    def part_arrival(z):
        return pltpu.make_async_remote_copy(
            src_ref=part_out.at[me_z],
            dst_ref=part_in.at[z],
            send_sem=part_sem.at[0, me_z, 0],
            recv_sem=part_sem.at[1, z, 0],
            device_id=(me_e, z * 2 + me_c),
            device_id_type=MESH,
        )

    keep_rows = pltpu.make_async_copy(
        rows_out.at[me_z, me_e], rows_in.at[me_z, me_e], local_sem.at[0]
    )
    keep_gate = pltpu.make_async_copy(gate_out.at[me_e], gate_in.at[me_e], local_sem.at[1])
    keep_score = pltpu.make_async_copy(score_out.at[me_e], score_in.at[me_e], local_sem.at[2])

    half = me_z // 2
    partner = me_z + 1 - 2 * (me_z % 2)
    across = [3 * (1 - half), 2 - half]

    def send_rows(i):
        if relayed:
            z = [*across, partner, me_z][i]
        else:
            z = lax.rem(me_z + i + 1, chips)
        block = jnp.dot(
            chosen16,
            grad_v[:, pl.ds(pl.multiple_of(z * cols, cols), cols)],
            preferred_element_type=F32,
        )
        rows_out[z] = block.astype(BF16).reshape(ep, cap, cols)

        def one(k):
            e = lax.rem(me_e + k, ep)

            @pl.when((e != me_e) | (z != me_z))
            def _():
                row_copy(e, z).start()

        loop(ep, one)

    loop(chips, send_rows)
    w_copy.start()
    keep_rows.start()
    keep_gate.start()

    @pl.loop(1, ep)
    def _(k):
        gate_copy(lax.rem(me_e + k, ep)).start()

    load_saved.wait()
    block_rows = 16

    @pl.loop(0, slots // block_rows)
    def _(i):
        at = pl.ds(pl.multiple_of(i * block_rows, block_rows), block_rows)
        a = saved_v[at, :ff].astype(F32)
        u = saved_v[at, ff:].astype(F32)
        sig = jax.nn.sigmoid(a)
        silu = a * sig
        hid[at, :] = (silu * u).astype(BF16)
        fa[at, :] = u * sig * (1.0 + a * (1.0 - sig))
        fu[at, :] = silu

    load_w.wait()
    w_copy.wait()

    def times_w(z):
        rows = rows_in[z].reshape(slots, cols)
        return lax.dot_general(
            rows[:, :kw], wbuf[0], nt, preferred_element_type=F32
        ) + lax.dot_general(rows[:, kw:], wbuf[1], nt, preferred_element_type=F32)

    def wait_rows(z):
        def one(k):
            e = lax.rem(me_e + k, ep)

            @pl.when((e != me_e) | (z != me_z))
            def _():
                row_arrival(e, z).wait_recv()

        loop(ep, one)

    piece = slots // 4

    def post(i, j, c, z):
        at = pl.ds(c * piece, piece)
        return pltpu.make_async_remote_copy(
            src_ref=part_out.at[i, at],
            dst_ref=part_in.at[j, at],
            send_sem=part_sem.at[0, i, c],
            recv_sem=part_sem.at[1, j, c],
            device_id=(me_e, z * 2 + me_c),
            device_id_type=MESH,
        )

    def relay_parts():
        edge = me_z % 3 == 0

        def send_partner():
            wait_rows(partner)
            part_out[2] = times_w(partner).astype(BF16)
            for c in range(4):
                post(2, 0, c, partner).start()

            wait_rows(me_z)
            keep_rows.wait()
            own[...] = times_w(me_z)

        pl.when(jnp.logical_not(edge))(send_partner)
        for i in range(2):
            wait_rows(across[i])
            tmp[...] = times_w(across[i])
            for c in range(4):
                at = pl.ds(c * piece, piece)

                @pl.when(edge)
                def _():
                    part_out[i, at, :] = tmp[at, :].astype(BF16)
                    post(i, 2 + i, c, partner).start()

                @pl.when(jnp.logical_not(edge))
                def _():
                    post(i, 2 + i, c, partner).wait_recv()
                    total = tmp[at, :] + part_in[2 + i, at, :].astype(F32)
                    part_out[i, at, :] = total.astype(BF16)
                    post(i, 1, c, across[i]).start()

        pl.when(edge)(send_partner)
        for j in range(2):
            for c in range(4):
                at = pl.ds(c * piece, piece)
                post(2, j, c, partner).wait_recv()
                own[at, :] += part_in[j, at, :].astype(F32)

    if relayed:
        relay_parts()
    else:
        def send_part(i):
            z = lax.rem(me_z + chips - 1 - i, chips)
            wait_rows(z)
            part_out[z] = times_w(z).astype(BF16)
            part_copy(z).start()

        loop(chips - 1, send_part)
        wait_rows(me_z)
        keep_rows.wait()
        own[...] = times_w(me_z)

        def add_part(i):
            z = lax.rem(me_z + i + 1, chips)
            part_arrival(z).wait_recv()

            @pl.loop(0, slots // block_rows)
            def _(j):
                at = pl.ds(pl.multiple_of(j * block_rows, block_rows), block_rows)
                own[at, :] += part_in[z, at, :].astype(F32)

        loop(chips - 1, add_part)

    keep_gate.wait()

    @pl.loop(1, ep)
    def _(k):
        gate_arrival(lax.rem(me_e + k, ep)).wait_recv()

    @pl.loop(0, ep)
    def _(e):
        at = pl.ds(pl.multiple_of(e * cap, cap), cap)
        score = jnp.sum(own[at, :] * hid[at, :].astype(F32), axis=1, keepdims=True)
        score_out[e] = jnp.broadcast_to(score, (cap, 128))

    @pl.loop(1, ep)
    def _(k):
        score_copy(lax.rem(me_e + k, ep)).start()

    keep_score.start()

    @pl.loop(0, ep)
    def _(e):
        at = pl.ds(pl.multiple_of(e * cap, cap), cap)
        scaled = own[at, :] * gate_in[e][:, :1]
        pre_v[at, :ff] = (scaled * fa[at, :]).astype(BF16)
        pre_v[at, ff:] = (scaled * fu[at, :]).astype(BF16)

    store = pltpu.make_async_copy(pre_v, pre_ref, load_sem.at[0])
    store.start()

    keep_score.wait()

    @pl.loop(1, ep)
    def _(k):
        score_arrival(lax.rem(me_e + k, ep)).wait_recv()

    got = score_in[...].reshape(slots, 128)
    spread = jnp.sum((chosen * got[:, :1]).reshape(ep, cap, tokens), axis=1)
    result = jnp.zeros((top, tokens), F32)
    for f in range(ep):
        result += jnp.where(routes == f * step, spread[f : f + 1, :], 0.0)
    gg_ref[...] = result

    def sent(k):
        e = lax.rem(me_e + k // chips, ep)
        z = lax.rem(me_z + k % chips, chips)
        row_copy(e, z).wait_send()

    @pl.loop(1, ep * chips)
    def _(k):
        sent(k)

    @pl.loop(1, ep)
    def _(k):
        e = lax.rem(me_e + k, ep)
        gate_copy(e).wait_send()
        score_copy(e).wait_send()

    if relayed:
        for i in range(3):
            for c in range(4):
                post(i, 0, c, partner).wait_send()
    else:

        @pl.loop(1, chips)
        def _(k):
            part_copy(lax.rem(me_z + k, chips)).wait_send()

    store.wait()


def on_device(ep, sp, grad_out, routes, gate, saved, w_down):
    tokens, width = grad_out.shape
    slots = saved.shape[2]
    ff = saved.shape[3] // 2
    kw = w_down.shape[2]
    cap = slots // ep
    chips = sp // 2
    cols = 2 * kw
    vmem = pl.BlockSpec(memory_space=pltpu.VMEM)
    hbm = pl.BlockSpec(memory_space=pl.ANY)
    pre, grad_gate = pl.pallas_call(
        functools.partial(kernel, ep, chips),
        out_shape=(
            jax.ShapeDtypeStruct((slots, 2 * ff), BF16),
            jax.ShapeDtypeStruct((routes.shape[1], tokens), F32),
        ),
        in_specs=[vmem, vmem, hbm, hbm, hbm],
        out_specs=(hbm, vmem),
        scratch_shapes=[
            pltpu.VMEM((tokens, width), BF16),
            pltpu.VMEM((slots, 2 * ff), BF16),
            pltpu.VMEM((2, ff, kw), BF16),
            pltpu.VMEM((chips, ep, cap, cols), BF16),
            pltpu.VMEM((chips, ep, cap, cols), BF16),
            pltpu.VMEM((ep, cap, 128), F32),
            pltpu.VMEM((ep, cap, 128), F32),
            pltpu.VMEM((chips, slots, ff), BF16),
            pltpu.VMEM((chips, slots, ff), BF16),
            pltpu.VMEM((ep, cap, 128), F32),
            pltpu.VMEM((ep, cap, 128), F32),
            pltpu.VMEM((slots, ff), F32),
            pltpu.VMEM((slots, ff), F32),
            pltpu.VMEM((slots, ff), BF16),
            pltpu.VMEM((slots, ff), F32),
            pltpu.VMEM((slots, ff), F32),
            pltpu.VMEM((slots, 2 * ff), BF16),
            pltpu.SemaphoreType.DMA((3,)),
            pltpu.SemaphoreType.DMA((2,)),
            pltpu.SemaphoreType.DMA((2, chips, ep)),
            pltpu.SemaphoreType.DMA((2, ep)),
            pltpu.SemaphoreType.DMA((2, chips, 4)),
            pltpu.SemaphoreType.DMA((2, ep)),
            pltpu.SemaphoreType.DMA((3,)),
        ],
        compiler_params=pltpu.CompilerParams(
            collective_id=0, has_side_effects=True, vmem_limit_bytes=56 * 1024 * 1024
        ),
    )(routes.T, gate.T, grad_out, saved.reshape(slots, 2 * ff), w_down.reshape(ff, kw))
    return pre.reshape(saved.shape), grad_gate.T


def solution(mesh):
    ep, sp = mesh.shape["ep"], mesh.shape["sp"]
    in_specs = (
        P(("ep", "sp"), None),
        P(("ep", "sp"), None),
        P(("ep", "sp"), None),
        P("ep", "sp", None, None),
        P("ep", None, "sp"),
    )
    out_specs = (P("ep", "sp", None, None), P(("ep", "sp"), None))
    return jax.shard_map(
        functools.partial(on_device, ep, sp),
        mesh=mesh,
        in_specs=in_specs,
        out_specs=out_specs,
        check_vma=False,
    )
```

```python
import functools

import jax
import jax.numpy as jnp
from jax import lax
from jax.experimental import pallas as pl
from jax.experimental.pallas import tpu as pltpu
from jax.sharding import PartitionSpec as P

EXPERTS = 128
MESH = pl.DeviceIdType.MESH
F32 = jnp.float32
BF16 = jnp.bfloat16


def loop(count, body):
    if count <= 4:
        for i in range(count):
            body(i)
    else:

        @pl.loop(0, count)
        def _(i):
            body(i)


def kernel(
    ep,
    chips,
    routes_ref,
    gate_ref,
    grad_ref,
    saved_ref,
    w_ref,
    pre_ref,
    gg_ref,
    grad_v,
    saved_v,
    wbuf,
    rows_out,
    rows_in,
    gate_out,
    gate_in,
    part_out,
    part_in,
    score_out,
    score_in,
    own,
    hid,
    fa,
    fu,
    pre_v,
    load_sem,
    w_sem,
    row_sem,
    gate_sem,
    part_sem,
    score_sem,
    local_sem,
):
    top, tokens = routes_ref.shape
    nt = (((1,), (1,)), ((), ()))
    relayed = chips == 4
    cap = rows_out.shape[2]
    cols = rows_out.shape[3]
    slots = ep * cap
    ff = w_ref.shape[0]
    kw = w_ref.shape[1]
    me_e = lax.axis_index("ep")
    me_s = lax.axis_index("sp")
    me_z = me_s // 2
    me_c = me_s % 2
    sibling = me_z * 2 + (1 - me_c)

    load_grad = pltpu.make_async_copy(grad_ref, grad_v, load_sem.at[0])
    load_grad.start()
    load_w = pltpu.make_async_copy(w_ref, wbuf.at[me_c], load_sem.at[1])
    load_w.start()
    load_saved = pltpu.make_async_copy(saved_ref, saved_v, load_sem.at[2])
    load_saved.start()

    barrier = pltpu.get_barrier_semaphore()
    pl.semaphore_signal(barrier, inc=1, device_id=(me_e, sibling), device_id_type=MESH)

    def greet(k):
        e = lax.rem(me_e + k // chips, ep)
        z = lax.rem(me_z + k % chips, chips)
        pl.semaphore_signal(barrier, inc=1, device_id=(e, z * 2 + me_c), device_id_type=MESH)

    @pl.loop(1, ep * chips)
    def _(k):
        greet(k)

    step = EXPERTS // ep
    routes = routes_ref[...]
    gates = gate_ref[...].astype(F32)
    slot_id = lax.broadcasted_iota(jnp.int32, (slots, tokens), 0)
    place_id = (slot_id % cap).astype(F32)
    members, weights = [], []
    for f in range(ep):
        hit = (routes == f * step).astype(F32)
        count = jnp.sum(hit, axis=0, keepdims=True)
        value = jnp.sum(hit * gates, axis=0, keepdims=True)
        members.append(jnp.broadcast_to(count, (cap, tokens)))
        weights.append(jnp.broadcast_to(value, (cap, tokens)))
    member = jnp.concatenate(members, axis=0)
    weight = jnp.concatenate(weights, axis=0)
    before = (
        lax.broadcasted_iota(jnp.int32, (tokens, tokens), 0)
        < lax.broadcasted_iota(jnp.int32, (tokens, tokens), 1)
    ).astype(F32)
    place = jnp.dot(member.astype(BF16), before.astype(BF16), preferred_element_type=F32)
    chosen = jnp.where((place == place_id) & (member > 0.5), 1.0, 0.0)
    picked = jnp.sum(chosen * weight, axis=1, keepdims=True)
    gate_out[...] = jnp.broadcast_to(picked, (slots, 128)).reshape(ep, cap, 128)
    chosen16 = chosen.astype(BF16)

    load_grad.wait()
    pl.semaphore_wait(barrier, ep * chips)

    w_copy = pltpu.make_async_remote_copy(
        src_ref=w_ref,
        dst_ref=wbuf.at[me_c],
        send_sem=w_sem.at[0],
        recv_sem=w_sem.at[1],
        device_id=(me_e, sibling),
        device_id_type=MESH,
    )

    def row_copy(e, z):
        return pltpu.make_async_remote_copy(
            src_ref=rows_out.at[z, e],
            dst_ref=rows_in.at[me_z, me_e],
            send_sem=row_sem.at[0, z, e],
            recv_sem=row_sem.at[1, me_z, me_e],
            device_id=(e, z * 2 + me_c),
            device_id_type=MESH,
        )

    def row_arrival(e, z):
        return pltpu.make_async_remote_copy(
            src_ref=rows_out.at[me_z, me_e],
            dst_ref=rows_in.at[z, e],
            send_sem=row_sem.at[0, me_z, me_e],
            recv_sem=row_sem.at[1, z, e],
            device_id=(e, z * 2 + me_c),
            device_id_type=MESH,
        )

    def gate_copy(e):
        return pltpu.make_async_remote_copy(
            src_ref=gate_out.at[e],
            dst_ref=gate_in.at[me_e],
            send_sem=gate_sem.at[0, e],
            recv_sem=gate_sem.at[1, me_e],
            device_id=(e, me_s),
            device_id_type=MESH,
        )

    def gate_arrival(e):
        return pltpu.make_async_remote_copy(
            src_ref=gate_out.at[me_e],
            dst_ref=gate_in.at[e],
            send_sem=gate_sem.at[0, me_e],
            recv_sem=gate_sem.at[1, e],
            device_id=(e, me_s),
            device_id_type=MESH,
        )

    def score_copy(e):
        return pltpu.make_async_remote_copy(
            src_ref=score_out.at[e],
            dst_ref=score_in.at[me_e],
            send_sem=score_sem.at[0, e],
            recv_sem=score_sem.at[1, me_e],
            device_id=(e, me_s),
            device_id_type=MESH,
        )

    def score_arrival(e):
        return pltpu.make_async_remote_copy(
            src_ref=score_out.at[me_e],
            dst_ref=score_in.at[e],
            send_sem=score_sem.at[0, me_e],
            recv_sem=score_sem.at[1, e],
            device_id=(e, me_s),
            device_id_type=MESH,
        )

    def part_copy(z):
        return pltpu.make_async_remote_copy(
            src_ref=part_out.at[z],
            dst_ref=part_in.at[me_z],
            send_sem=part_sem.at[0, z, 0],
            recv_sem=part_sem.at[1, me_z, 0],
            device_id=(me_e, z * 2 + me_c),
            device_id_type=MESH,
        )

    def part_arrival(z):
        return pltpu.make_async_remote_copy(
            src_ref=part_out.at[me_z],
            dst_ref=part_in.at[z],
            send_sem=part_sem.at[0, me_z, 0],
            recv_sem=part_sem.at[1, z, 0],
            device_id=(me_e, z * 2 + me_c),
            device_id_type=MESH,
        )

    keep_rows = pltpu.make_async_copy(
        rows_out.at[me_z, me_e], rows_in.at[me_z, me_e], local_sem.at[0]
    )
    keep_gate = pltpu.make_async_copy(gate_out.at[me_e], gate_in.at[me_e], local_sem.at[1])
    keep_score = pltpu.make_async_copy(score_out.at[me_e], score_in.at[me_e], local_sem.at[2])

    half = me_z // 2
    partner = me_z + 1 - 2 * (me_z % 2)
    across = [3 * (1 - half), 2 - half]

    def send_rows(i):
        if relayed:
            z = [*across, partner, me_z][i]
        else:
            z = lax.rem(me_z + i + 1, chips)
        block = jnp.dot(
            chosen16,
            grad_v[:, pl.ds(pl.multiple_of(z * cols, cols), cols)],
            preferred_element_type=F32,
        )
        rows_out[z] = block.astype(BF16).reshape(ep, cap, cols)

        def one(k):
            e = lax.rem(me_e + k, ep)

            @pl.when((e != me_e) | (z != me_z))
            def _():
                row_copy(e, z).start()

        loop(ep, one)

    loop(chips, send_rows)
    w_copy.start()
    keep_rows.start()
    keep_gate.start()

    @pl.loop(1, ep)
    def _(k):
        gate_copy(lax.rem(me_e + k, ep)).start()

    load_saved.wait()
    block_rows = 16

    @pl.loop(0, slots // block_rows)
    def _(i):
        at = pl.ds(pl.multiple_of(i * block_rows, block_rows), block_rows)
        a = saved_v[at, :ff].astype(F32)
        u = saved_v[at, ff:].astype(F32)
        sig = jax.nn.sigmoid(a)
        silu = a * sig
        hid[at, :] = (silu * u).astype(BF16)
        fa[at, :] = u * sig * (1.0 + a * (1.0 - sig))
        fu[at, :] = silu

    load_w.wait()
    w_copy.wait()

    def times_w(z):
        rows = rows_in[z].reshape(slots, cols)
        return lax.dot_general(
            rows[:, :kw], wbuf[0], nt, preferred_element_type=F32
        ) + lax.dot_general(rows[:, kw:], wbuf[1], nt, preferred_element_type=F32)

    def wait_rows(z):
        def one(k):
            e = lax.rem(me_e + k, ep)

            @pl.when((e != me_e) | (z != me_z))
            def _():
                row_arrival(e, z).wait_recv()

        loop(ep, one)

    piece = slots // 4

    def post(i, j, c, z):
        at = pl.ds(c * piece, piece)
        return pltpu.make_async_remote_copy(
            src_ref=part_out.at[i, at],
            dst_ref=part_in.at[j, at],
            send_sem=part_sem.at[0, i, c],
            recv_sem=part_sem.at[1, j, c],
            device_id=(me_e, z * 2 + me_c),
            device_id_type=MESH,
        )

    def relay_parts():
        edge = me_z % 3 == 0

        def send_partner():
            wait_rows(partner)
            part_out[2] = times_w(partner).astype(BF16)
            for c in range(4):
                post(2, 0, c, partner).start()

        pl.when(jnp.logical_not(edge))(send_partner)
        for i in range(2):
            wait_rows(across[i])
            own[...] = times_w(across[i])
            for c in range(4):
                at = pl.ds(c * piece, piece)

                @pl.when(edge)
                def _():
                    part_out[i, at, :] = own[at, :].astype(BF16)
                    post(i, 2 + i, c, partner).start()

                @pl.when(jnp.logical_not(edge))
                def _():
                    post(i, 2 + i, c, partner).wait_recv()
                    total = own[at, :] + part_in[2 + i, at, :].astype(F32)
                    part_out[i, at, :] = total.astype(BF16)
                    post(i, 1, c, across[i]).start()

        pl.when(edge)(send_partner)
        wait_rows(me_z)
        keep_rows.wait()
        own[...] = times_w(me_z)
        for c in range(4):
            at = pl.ds(c * piece, piece)
            post(2, 0, c, partner).wait_recv()
            post(2, 1, c, partner).wait_recv()
            total = own[at, :] + part_in[0, at, :].astype(F32)
            total += part_in[1, at, :].astype(F32)
            own[at, :] = total
            if piece == cap:
                score = jnp.sum(total * hid[at, :].astype(F32), axis=1, keepdims=True)
                score_out[c] = jnp.broadcast_to(score, (cap, 128))

                @pl.when(c != me_e)
                def _():
                    score_copy(c).start()


    if relayed:
        relay_parts()
    else:
        def send_part(i):
            z = lax.rem(me_z + chips - 1 - i, chips)
            wait_rows(z)
            part_out[z] = times_w(z).astype(BF16)
            part_copy(z).start()

        loop(chips - 1, send_part)
        wait_rows(me_z)
        keep_rows.wait()
        own[...] = times_w(me_z)

        def add_part(i):
            z = lax.rem(me_z + i + 1, chips)
            part_arrival(z).wait_recv()

            @pl.loop(0, slots // block_rows)
            def _(j):
                at = pl.ds(pl.multiple_of(j * block_rows, block_rows), block_rows)
                own[at, :] += part_in[z, at, :].astype(F32)

        loop(chips - 1, add_part)

    keep_gate.wait()

    @pl.loop(1, ep)
    def _(k):
        gate_arrival(lax.rem(me_e + k, ep)).wait_recv()

    if not (relayed and slots // 4 == cap):

        @pl.loop(0, ep)
        def _(e):
            at = pl.ds(pl.multiple_of(e * cap, cap), cap)
            score = jnp.sum(own[at, :] * hid[at, :].astype(F32), axis=1, keepdims=True)
            score_out[e] = jnp.broadcast_to(score, (cap, 128))

        @pl.loop(1, ep)
        def _(k):
            score_copy(lax.rem(me_e + k, ep)).start()

    keep_score.start()

    @pl.loop(0, ep)
    def _(e):
        at = pl.ds(pl.multiple_of(e * cap, cap), cap)
        scaled = own[at, :] * gate_in[e][:, :1]
        pre_v[at, :ff] = (scaled * fa[at, :]).astype(BF16)
        pre_v[at, ff:] = (scaled * fu[at, :]).astype(BF16)

    store = pltpu.make_async_copy(pre_v, pre_ref, load_sem.at[0])
    store.start()

    keep_score.wait()

    @pl.loop(1, ep)
    def _(k):
        score_arrival(lax.rem(me_e + k, ep)).wait_recv()

    got = score_in[...].reshape(slots, 128)
    spread = jnp.sum((chosen * got[:, :1]).reshape(ep, cap, tokens), axis=1)
    result = jnp.zeros((top, tokens), F32)
    for f in range(ep):
        result += jnp.where(routes == f * step, spread[f : f + 1, :], 0.0)
    gg_ref[...] = result

    def sent(k):
        e = lax.rem(me_e + k // chips, ep)
        z = lax.rem(me_z + k % chips, chips)
        row_copy(e, z).wait_send()

    @pl.loop(1, ep * chips)
    def _(k):
        sent(k)

    @pl.loop(1, ep)
    def _(k):
        e = lax.rem(me_e + k, ep)
        gate_copy(e).wait_send()
        score_copy(e).wait_send()

    if relayed:
        for i in range(3):
            for c in range(4):
                post(i, 0, c, partner).wait_send()
    else:

        @pl.loop(1, chips)
        def _(k):
            part_copy(lax.rem(me_z + k, chips)).wait_send()

    store.wait()


def on_device(ep, sp, grad_out, routes, gate, saved, w_down):
    tokens, width = grad_out.shape
    slots = saved.shape[2]
    ff = saved.shape[3] // 2
    kw = w_down.shape[2]
    cap = slots // ep
    chips = sp // 2
    cols = 2 * kw
    vmem = pl.BlockSpec(memory_space=pltpu.VMEM)
    hbm = pl.BlockSpec(memory_space=pl.ANY)
    pre, grad_gate = pl.pallas_call(
        functools.partial(kernel, ep, chips),
        out_shape=(
            jax.ShapeDtypeStruct((slots, 2 * ff), BF16),
            jax.ShapeDtypeStruct((routes.shape[1], tokens), F32),
        ),
        in_specs=[vmem, vmem, hbm, hbm, hbm],
        out_specs=(hbm, vmem),
        scratch_shapes=[
            pltpu.VMEM((tokens, width), BF16),
            pltpu.VMEM((slots, 2 * ff), BF16),
            pltpu.VMEM((2, ff, kw), BF16),
            pltpu.VMEM((chips, ep, cap, cols), BF16),
            pltpu.VMEM((chips, ep, cap, cols), BF16),
            pltpu.VMEM((ep, cap, 128), F32),
            pltpu.VMEM((ep, cap, 128), F32),
            pltpu.VMEM((chips, slots, ff), BF16),
            pltpu.VMEM((chips, slots, ff), BF16),
            pltpu.VMEM((ep, cap, 128), F32),
            pltpu.VMEM((ep, cap, 128), F32),
            pltpu.VMEM((slots, ff), F32),
            pltpu.VMEM((slots, ff), BF16),
            pltpu.VMEM((slots, ff), F32),
            pltpu.VMEM((slots, ff), F32),
            pltpu.VMEM((slots, 2 * ff), BF16),
            pltpu.SemaphoreType.DMA((3,)),
            pltpu.SemaphoreType.DMA((2,)),
            pltpu.SemaphoreType.DMA((2, chips, ep)),
            pltpu.SemaphoreType.DMA((2, ep)),
            pltpu.SemaphoreType.DMA((2, chips, 4)),
            pltpu.SemaphoreType.DMA((2, ep)),
            pltpu.SemaphoreType.DMA((3,)),
        ],
        compiler_params=pltpu.CompilerParams(
            collective_id=0, has_side_effects=True, vmem_limit_bytes=56 * 1024 * 1024
        ),
    )(routes.T, gate.T, grad_out, saved.reshape(slots, 2 * ff), w_down.reshape(ff, kw))
    return pre.reshape(saved.shape), grad_gate.T


def solution(mesh):
    ep, sp = mesh.shape["ep"], mesh.shape["sp"]
    in_specs = (
        P(("ep", "sp"), None),
        P(("ep", "sp"), None),
        P(("ep", "sp"), None),
        P("ep", "sp", None, None),
        P("ep", None, "sp"),
    )
    out_specs = (P("ep", "sp", None, None), P(("ep", "sp"), None))
    return jax.shard_map(
        functools.partial(on_device, ep, sp),
        mesh=mesh,
        in_specs=in_specs,
        out_specs=out_specs,
        check_vma=False,
    )
```
